256 devices in a mesh: dp: 8 (over x, core), head: 32 (over y, z).
Axes of the slice: x: 4, y: 4, z: 8, core: 2. Of those that a mesh axis runs over, the one named last changes fastest.
Arguments:
- q_latent: bfloat16 [512, 1536], P('dp'), may hold values from -6 to 6
- w_qnope: bfloat16 [1536, 16384], P('dp', 'head'), may hold values from -0.15625 to 0.15625
- w_qrope: bfloat16 [1536, 8192], P('dp', 'head'), may hold values from -0.15625 to 0.15625
- w_uk: bfloat16 [128, 128, 512], P('head'), may hold values from -0.5 to 0.5
- w_uv: bfloat16 [128, 512, 128], P('head'), may hold values from -0.25 to 0.25
- w_out: bfloat16 [128, 128, 7168], P('head', 'dp'), may hold values from -0.09375 to 0.09375
- cache_latent: bfloat16 [16384, 128, 512], P(('dp', 'head')), may hold values from -210 to 210
- cache_rope: bfloat16 [16384, 64, 128], P(('dp', 'head')), may hold values from -6 to 6
- new_latent: bfloat16 [512, 512], P(('dp', 'head')), may hold values from -6 to 6
- new_rope: bfloat16 [512, 64], P(('dp', 'head')), may hold values from -6 to 6
- lengths: int32 [512], P('dp'), may hold values from 1 to 4096, as said below
- page_table: int32 [512, 32], P(('dp', 'head')), may hold values from 0 to 63, as said below
Outputs:
- mixed: bfloat16 [512, 7168], P('dp', 'head')
The draws below stay inside these ranges and needn't reach their ends.
Inputs may be any that keep to these rules, and one draw needn't show every extreme that they name: `lengths`: each row of one device has at most 4096 cached tokens; some row holds exactly 4096. `page_table`: the entries of the 2 rows of one device together name each of its 64 pool pages once.
All inputs are finite; a program needn't handle non-finite values.
Results may differ from the reference program's by a relative error of at most 0.022.
Values may be sent and summed in bfloat16 or wider, within the bound.
No kernel may reach another device: no remote copies, remote signals or barrier semaphores. Data moves between devices by JAX's collectives and lax.ppermute only.
A program may use at most 128 MiB of HBM per device.

```python
import jax
import jax.numpy as jnp
from jax import lax

D = 7168
QR = 1536
LAT = 512
ROPE = 64
NOPE = 128
VDIM = 128
HEADS = 128
PAGE = 128
PAGES_ROW = 32
ROW_DEV = 2
ROWS = 512
MAXLEN = 4096
POOL = 16384


def draw_cache_latent(key, part):
    key = jax.random.fold_in(key, 13)
    first = jax.random.fold_in(key, 0)
    shape = (POOL, PAGE, LAT)
    return jnp.clip(jax.random.normal(first, shape, jnp.float32), -6.0, 6.0).astype(jnp.bfloat16)


def draw_lengths(key, part):
    key = jax.random.fold_in(key, 11)
    first, second, third = jax.random.split(key, 3)
    owners = ROWS // ROW_DEV
    page_caps = jax.random.randint(first, (owners, 1), 1, PAGES_ROW + 1)
    raw = jax.random.randint(second, (owners, ROW_DEV), 0, 1 << 30)
    counts = (1 + raw % (page_caps * PAGE)).reshape(ROWS)
    longest = jax.random.randint(third, (), 0, ROWS)
    counts = jnp.where(jnp.arange(ROWS) == longest, PAGES_ROW * PAGE, counts)
    return counts.astype(jnp.int32)


def draw_page_table(key, part):
    key = jax.random.fold_in(key, 12)
    owners = ROWS // ROW_DEV
    keys = jax.random.split(key, owners)
    perms = jax.vmap(lambda single: jax.random.permutation(single, ROW_DEV * PAGES_ROW))(keys)
    return perms.reshape(ROWS, PAGES_ROW).astype(jnp.int32)


def with_spikes(values, stream_key, source, target, shards_of, factor):
    owner, partner = [(jnp.arange(values.shape[dim]) // (values.shape[dim] // shards_of)).reshape([-1 if axis == dim else 1 for axis in range(values.ndim)]) for dim in (source, target)]
    chosen = jax.random.permutation(stream_key, shards_of)[partner]
    strong = (owner == chosen) | (owner == (partner + shards_of // 2) % shards_of)
    return jnp.where(strong, factor * values, values)


def levels(key, shape, pieces, low, largest):
    def one(axis_at, blocks):
        draws = jax.random.uniform(jax.random.fold_in(jax.random.fold_in(key, 6), axis_at), (blocks,), jnp.float32, low / len(pieces), largest / len(pieces))
        return jnp.repeat(jnp.exp(draws), shape[axis_at] // blocks).reshape((-1,) + (1,) * (len(shape) - axis_at - 1))

    loudness = one(*pieces[0])
    for cut in pieces[1:]:
        loudness = loudness * one(*cut)
    return loudness


def noise(own_key, extent, spread, most, cuts=(), kind=jnp.bfloat16):
    level = levels(own_key, extent, cuts, -0.22, 0.18) if cuts else 1.0
    array = jax.random.normal(own_key, extent, jnp.float32) * spread * level
    return jnp.minimum(jnp.maximum(array, -most), most).astype(kind)


def heavy_noise(own_key, extent, width, limit, cuts, heavy, kind=jnp.bfloat16):
    values = width * jax.random.normal(own_key, extent, jnp.float32)
    if cuts:
        values = values * levels(own_key, extent, cuts, -0.22, 0.18)
    return jnp.clip(with_spikes(values, jax.random.fold_in(own_key, 3), *heavy), -limit, limit).astype(kind)


def setup_inputs(seed: int = 0) -> dict:
    streams_of = jax.random.split(jax.random.key(seed), 13)
    return {
        "q_latent": noise(streams_of[0], (ROWS, QR), 1.0, 6.0, ((0, 8),)),
        "w_qnope": noise(streams_of[1], (QR, HEADS * NOPE), QR ** -0.5, 0.15625, ((0, 8), (1, 32))),
        "w_qrope": noise(streams_of[2], (QR, HEADS * ROPE), QR ** -0.5, 0.15625, ((0, 8), (1, 32))),
        "w_uk": noise(streams_of[3], (HEADS, NOPE, LAT), NOPE ** -0.5, 0.5, ((0, 32),)),
        "w_uv": noise(streams_of[4], (HEADS, LAT, VDIM), LAT ** -0.5, 0.25, ((0, 32),)),
        "w_out": heavy_noise(streams_of[5], (HEADS, VDIM, D), (HEADS * VDIM) ** -0.5, 0.09375, ((0, 32), (1, 8)), (0, 2, 32, 2.75)),
        "cache_latent": draw_cache_latent(jax.random.fold_in(streams_of[12], 71), 0),
        "cache_rope": noise(streams_of[7], (POOL, ROPE, PAGE), 1.0, 6.0, ((0, 256),)),
        "new_latent": noise(streams_of[8], (ROWS, LAT), 1.0, 6.0, ((0, 256),)),
        "new_rope": noise(streams_of[9], (ROWS, ROPE), 1.0, 6.0, ((0, 256),)),
        "lengths": draw_lengths(jax.random.fold_in(streams_of[12], 71), 0),
        "page_table": draw_page_table(jax.random.fold_in(streams_of[12], 71), 0),
    }


def rotate(x, pos):
    half = x.shape[-1] // 2
    freq = 10000.0 ** (-2.0 * jnp.arange(half, dtype=jnp.float32) / (2 * half))
    angle = pos.astype(jnp.float32)[:, None, None] * freq
    first = x[..., :half]
    second = x[..., half:]
    return jnp.concatenate([first * jnp.cos(angle) - second * jnp.sin(angle), second * jnp.cos(angle) + first * jnp.sin(angle)], axis=-1)


def reference(q_latent, w_qnope, w_qrope, w_uk, w_uv, w_out, cache_latent, cache_rope, new_latent, new_rope, lengths, page_table):
    scale = 1.0 / (NOPE + ROPE) ** 0.5
    q_nope = jnp.dot(q_latent, w_qnope, preferred_element_type=jnp.float32).astype(jnp.bfloat16).reshape(ROWS, HEADS, NOPE)
    q_abs = jnp.einsum("rhn,hnl->rhl", q_nope.astype(jnp.float32), w_uk.astype(jnp.float32), precision=lax.Precision.HIGHEST).astype(jnp.bfloat16)
    q_pe = jnp.dot(q_latent, w_qrope, preferred_element_type=jnp.float32).reshape(ROWS, HEADS, ROPE)
    q_rot = rotate(q_pe, lengths).astype(jnp.bfloat16)
    owner = (jnp.arange(ROWS) // ROW_DEV).astype(jnp.int32)
    global_pages = (page_table + owner[:, None] * (ROW_DEV * PAGES_ROW)).astype(jnp.int32)

    def one_row(items):
        query_abs, query_rot, pages, length, latent_new, rope_new = items
        latent = cache_latent[pages].reshape(MAXLEN, LAT).astype(jnp.float32)
        rope_keys = jnp.transpose(cache_rope[pages], (1, 0, 2)).reshape(ROPE, MAXLEN).astype(jnp.float32)
        qa = query_abs.astype(jnp.float32)
        qr = query_rot.astype(jnp.float32)
        scores = (jnp.dot(qa, latent.T, precision=lax.Precision.HIGHEST) + jnp.dot(qr, rope_keys, precision=lax.Precision.HIGHEST)) * scale
        position = jnp.arange(MAXLEN)
        scores = jnp.where(position[None, :] < length, scores, -jnp.inf)
        score_new = (jnp.dot(qa, latent_new.astype(jnp.float32), precision=lax.Precision.HIGHEST) + jnp.dot(qr, rope_new.astype(jnp.float32), precision=lax.Precision.HIGHEST)) * scale
        top = jnp.maximum(jnp.max(scores, axis=1), score_new)
        weights = jnp.exp(scores - top[:, None])
        weight_new = jnp.exp(score_new - top)
        total = jnp.sum(weights, axis=1) + weight_new
        probs = (weights / total[:, None]).astype(jnp.bfloat16).astype(jnp.float32)
        prob_new = (weight_new / total).astype(jnp.bfloat16).astype(jnp.float32)
        summed = jnp.dot(probs, latent, precision=lax.Precision.HIGHEST) + prob_new[:, None] * latent_new.astype(jnp.float32)[None, :]
        return summed.astype(jnp.bfloat16)

    attn = lax.map(one_row, (q_abs, q_rot, global_pages, lengths, new_latent, new_rope))
    values = jnp.einsum("rhl,hlv->rhv", attn.astype(jnp.float32), w_uv.astype(jnp.float32), precision=lax.Precision.HIGHEST).astype(jnp.bfloat16)
    mixed = jnp.dot(values.reshape(ROWS, HEADS * VDIM), w_out.reshape(HEADS * VDIM, D), preferred_element_type=jnp.float32)
    return mixed.astype(jnp.bfloat16)
```

```python
import math

import jax
import jax.numpy as jnp
from jax import lax
from jax.experimental import pallas as pl
from jax.experimental.pallas import tpu as pltpu
from jax.sharding import PartitionSpec as P

BLOCK_PAGES = 8
Y = 4
Z = 8
Z_GROUPS = [[y * Z + z for z in range(Z)] for y in range(Y)]
Y_GROUPS = [[y * Z + z for y in range(Y)] for z in range(Z)]
F32 = jnp.float32
BF16 = jnp.bfloat16
WHOLE = pl.BlockSpec(memory_space=pltpu.VMEM)
SCALARS = pl.BlockSpec(memory_space=pltpu.SMEM)
IN_PLACE = pl.BlockSpec(memory_space=pl.ANY)


def dot(a, b):
    return jnp.dot(a, b, preferred_element_type=F32)


def params():
    return pltpu.CompilerParams(vmem_limit_bytes=40 * 1024 * 1024)


def project_kernel(pieces, latent_ref, *refs):
    piece_refs = refs[:pieces]
    uk_ref, cos_ref, sin_ref, out_ref = refs[pieces:]
    heads, nope_dim, width = uk_ref.shape
    both = None
    for i in range(pieces):
        term = dot(latent_ref[i], piece_refs[i][...])
        both = term if both is None else both + term
    query = both[:, : heads * nope_dim].astype(BF16)
    for j in range(heads):
        part = dot(query[:, j * nope_dim : (j + 1) * nope_dim], uk_ref[j])
        out_ref[:, j * width : (j + 1) * width] = part.astype(BF16)
    turned = both[:, heads * nope_dim :]
    lanes = turned.shape[1]
    rope_dim = lanes // heads
    lane = lax.broadcasted_iota(jnp.int32, turned.shape, 1)
    half = rope_dim // 2
    swapped = jnp.where(
        lane % rope_dim < half,
        pltpu.roll(turned, lanes - half, 1),
        pltpu.roll(turned, half, 1),
    )
    rotated = turned * cos_ref[...] + swapped * sin_ref[...]
    out_ref[:, heads * width :] = rotated.astype(BF16)


def project(latent, pieces, w_uk, cos, sin):
    heads, _, width = w_uk.shape
    rows = latent.shape[1]

    def kernel(*refs):
        project_kernel(len(pieces), *refs)

    return pl.pallas_call(
        kernel,
        out_shape=jax.ShapeDtypeStruct((rows, heads * width + cos.shape[1]), BF16),
        in_specs=[WHOLE] * (4 + len(pieces)),
        out_specs=WHOLE,
        compiler_params=params(),
        name="project",
    )(latent, *pieces, w_uk, cos, sin)


def sorter(rows, own, transposed):
    a = lax.broadcasted_iota(jnp.int32, (rows, rows), 0)
    b = lax.broadcasted_iota(jnp.int32, (rows, rows), 1)
    if transposed:
        a, b = b, a
    sources = rows // own
    return ((a % sources) * own + a // sources == b).astype(F32).astype(BF16)


def attend_kernel(
    length_ref, table_ref, query_ref, new_ref, new_rope_ref, latent_hbm, rope_hbm, out_ref,
    latents, ropes, latent_sem, rope_sem,
):
    own, blocks, keys, width = latents.shape
    rope_dim = ropes.shape[2]
    page = latent_hbm.shape[1]
    pages = keys // page
    rows = query_ref.shape[0]
    sources = rows // own
    heads = (query_ref.shape[1]) // (width + rope_dim)
    nope_rope = 128 + rope_dim
    factor = math.log2(math.e) / nope_rope**0.5
    for b in range(blocks):
        for r in range(own):
            for p in range(pages):
                index = table_ref[r, b * pages + p]
                span = pl.ds(p * page, page)
                pltpu.make_async_copy(
                    latent_hbm.at[index], latents.at[r, b, span], latent_sem.at[r, b]
                ).start()
                pltpu.make_async_copy(
                    rope_hbm.at[index], ropes.at[r, b, :, span], rope_sem.at[r, b]
                ).start()
    ordered = dot(sorter(rows, own, False), query_ref[...]).astype(BF16)
    absorbed, rotary, top, total, summed = [], [], [], [], []
    for r in range(own):
        part = ordered[r * sources : (r + 1) * sources]
        q_abs = jnp.concatenate(
            [part[:, j * width : (j + 1) * width] for j in range(heads)], axis=0
        )
        start = heads * width
        q_rot = jnp.concatenate(
            [part[:, start + j * rope_dim : start + (j + 1) * rope_dim] for j in range(heads)],
            axis=0,
        )
        new = new_ref[r : r + 1, :].astype(F32)
        new_rope = new_rope_ref[r : r + 1, :].astype(F32)
        score = jnp.sum(q_abs.astype(F32) * new, axis=1, keepdims=True)
        score += jnp.sum(q_rot.astype(F32) * new_rope, axis=1, keepdims=True)
        absorbed.append(q_abs)
        rotary.append(q_rot)
        top.append(score * factor)
        total.append(jnp.ones_like(score))
        summed.append(jnp.broadcast_to(new, q_abs.shape))
    for b in range(blocks):
        for r in range(own):
            pltpu.make_async_copy(latents.at[r, b], latents.at[r, b], latent_sem.at[r, b]).wait()
            pltpu.make_async_copy(ropes.at[r, b], ropes.at[r, b], rope_sem.at[r, b]).wait()
        for r in range(own):
            block = latents[r, b]
            scores = lax.dot_general(
                absorbed[r], block, (((1,), (1,)), ((), ())), preferred_element_type=F32
            )
            scores = (scores + dot(rotary[r], ropes[r, b])) * factor
            position = b * keys + lax.broadcasted_iota(jnp.int32, scores.shape, 1)
            scores = jnp.where(position < length_ref[r], scores, -jnp.inf)
            highest = jnp.maximum(top[r], jnp.max(scores, axis=1, keepdims=True))
            fade = jnp.exp2(top[r] - highest)
            weights = jnp.exp2(scores - highest)
            total[r] = total[r] * fade + jnp.sum(weights, axis=1, keepdims=True)
            summed[r] = summed[r] * fade + dot(weights.astype(BF16), block)
            top[r] = highest
    done = [(summed[r] / total[r]).astype(BF16) for r in range(own)]
    back = sorter(rows, own, True)
    for j in range(heads):
        piece = jnp.concatenate([d[j * sources : (j + 1) * sources] for d in done], axis=0)
        out_ref[:, j * width : (j + 1) * width] = dot(back, piece).astype(BF16)


def attend(lengths, table, query, new_latent, new_rope, cache_latent, cache_rope):
    own, slots = table.shape
    _, page, width = cache_latent.shape
    rope_dim = cache_rope.shape[1]
    blocks = slots // BLOCK_PAGES
    keys = BLOCK_PAGES * page
    heads = query.shape[1] // (width + rope_dim)
    return pl.pallas_call(
        attend_kernel,
        out_shape=jax.ShapeDtypeStruct((query.shape[0], heads * width), BF16),
        in_specs=[SCALARS, SCALARS, WHOLE, WHOLE, WHOLE, IN_PLACE, IN_PLACE],
        out_specs=WHOLE,
        scratch_shapes=[
            pltpu.VMEM((own, blocks, keys, width), BF16),
            pltpu.VMEM((own, blocks, rope_dim, keys), BF16),
            pltpu.SemaphoreType.DMA((own, blocks)),
            pltpu.SemaphoreType.DMA((own, blocks)),
        ],
        compiler_params=params(),
        name="attend",
    )(lengths, table, query, new_latent, new_rope, cache_latent, cache_rope)


def values_kernel(parts, attn_ref, uv_ref, out_ref):
    heads, width, value_dim = uv_ref.shape
    per = value_dim // parts
    columns = heads * value_dim
    source = lax.broadcasted_iota(jnp.int32, (value_dim, columns), 0)
    column = lax.broadcasted_iota(jnp.int32, (value_dim, columns), 1)
    total = None
    for j in range(heads):
        value = dot(attn_ref[:, j * width : (j + 1) * width], uv_ref[j]).astype(BF16)
        place = (source // per) * (heads * per) + j * per + source % per
        spread = dot(value, (column == place).astype(F32).astype(BF16))
        total = spread if total is None else total + spread
    out_ref[...] = total.astype(BF16)


def project_values(attn, w_uv, parts):
    heads, _, value_dim = w_uv.shape

    def kernel(*refs):
        values_kernel(parts, *refs)

    return pl.pallas_call(
        kernel,
        out_shape=jax.ShapeDtypeStruct((attn.shape[0], heads * value_dim), BF16),
        in_specs=[WHOLE] * 2,
        out_specs=WHOLE,
        compiler_params=params(),
        name="values",
    )(attn, w_uv)


def mix_kernel(values_ref, weights_ref, out_ref, sorted_ref, total_ref):
    step = pl.program_id(0)
    _, sources, per, columns = weights_ref.shape

    @pl.when(step == 0)
    def _():
        for d in range(sorted_ref.shape[0]):
            for y in range(sources):
                sorted_ref[d, :, y * per : (y + 1) * per] = values_ref[
                    y, :, d * per : (d + 1) * per
                ]
        total_ref[...] = jnp.zeros_like(total_ref)

    total_ref[...] += dot(sorted_ref[step], weights_ref[0].reshape(sources * per, columns))

    @pl.when(step == pl.num_programs(0) - 1)
    def _():
        parts, _, width = out_ref.shape
        for z in range(parts):
            out_ref[z] = total_ref[:, z * width : (z + 1) * width].astype(BF16)


def mix(values, weights, parts):
    sources, rows, _ = values.shape
    steps, _, per, columns = weights.shape
    return pl.pallas_call(
        mix_kernel,
        grid=(steps,),
        out_shape=jax.ShapeDtypeStruct((parts, rows, columns // parts), BF16),
        in_specs=[
            pl.BlockSpec(values.shape, lambda d: (0, 0, 0)),
            pl.BlockSpec((1, sources, per, columns), lambda d: (d, 0, 0, 0)),
        ],
        out_specs=pl.BlockSpec((parts, rows, columns // parts), lambda d: (0, 0, 0)),
        scratch_shapes=[
            pltpu.VMEM((steps, rows, sources * per), BF16),
            pltpu.VMEM((rows, columns), F32),
        ],
        compiler_params=params(),
        name="mix",
    )(values, weights)


def shift_dp(x, along, across):
    count = lax.axis_size("dp")
    chips = count // 2
    pairs = [
        (p * 2 + c, ((p + along) % chips) * 2 + (c ^ across)) for p in range(chips) for c in range(2)
    ]
    return lax.ppermute(x, "dp", pairs)


def gather_pieces(x):
    half = x.shape[0] // 2
    after, before, other = shift_dp(x, 1, 0), shift_dp(x, 3, 0), shift_dp(x, 0, 1)
    far_top, far_low = shift_dp(after[:half], 1, 0), shift_dp(before[half:], 3, 0)
    far = jnp.concatenate([far_top, far_low], axis=0)
    pieces = [x, other, after, shift_dp(after, 0, 1), before, shift_dp(before, 0, 1)]
    pieces += [far, shift_dp(far, 0, 1)]
    return pieces, [(0, 0), (0, 1), (1, 0), (1, 1), (3, 0), (3, 1), (2, 0), (2, 1)]


def angles(lengths, rope_dim, heads):
    half = rope_dim // 2
    freq = 10000.0 ** (-2.0 * jnp.arange(half, dtype=F32) / (2 * half))
    angle = lengths.astype(F32)[:, None] * freq
    cos, sin = jnp.cos(angle), jnp.sin(angle)
    cos = jnp.tile(cos, (1, 2 * heads))
    sin = jnp.tile(jnp.concatenate([-sin, sin], axis=1), (1, heads))
    return cos, sin


def body(
    q_latent,
    w_qnope,
    w_qrope,
    w_uk,
    w_uv,
    w_out,
    cache_latent,
    cache_rope,
    new_latent,
    new_rope,
    lengths,
    page_table,
):
    rows = q_latent.shape[0]
    heads, value_dim = w_uk.shape[0], w_uv.shape[2]
    own = page_table.shape[0]
    width_all = w_out.shape[2]
    dp_count = lax.axis_size("dp")
    sources = lax.axis_size("head")
    depth = w_out.shape[0] * w_out.shape[1]

    panel = w_out.reshape(depth, Y, width_all // Y).transpose(1, 0, 2)
    panel = lax.all_to_all(panel, "head", 0, 0, tiled=True, axis_index_groups=Y_GROUPS)
    panel = lax.all_gather(panel, "dp", axis=0)

    pieces, origins = gather_pieces(jnp.concatenate([w_qnope, w_qrope], axis=1))
    me = lax.axis_index("dp")
    chips = dp_count // 2
    order = jnp.stack(
        [((me // 2 - along) % chips) * 2 + (me % 2 + across) % 2 for along, across in origins]
    )
    latent = q_latent.reshape(rows, dp_count, -1).transpose(1, 0, 2)[order]
    cos, sin = angles(lengths, cache_rope.shape[1], heads)
    query = project(latent, pieces, w_uk, cos, sin)

    query = query.reshape(sources, own, query.shape[1])
    query = lax.all_to_all(query, "head", 0, 0, tiled=True).reshape(rows, -1)
    own_lengths = lax.dynamic_slice_in_dim(lengths, lax.axis_index("head") * own, own)
    attn = attend(own_lengths, page_table, query, new_latent, new_rope, cache_latent, cache_rope)
    attn = attn.reshape(sources, own, attn.shape[1])
    attn = lax.all_to_all(attn, "head", 0, 0, tiled=True).reshape(rows, -1)
    values = project_values(attn, w_uv, dp_count)
    values = jnp.broadcast_to(values[None], (Y, rows, heads * value_dim))
    values = lax.all_to_all(values, "head", 0, 0, tiled=True, axis_index_groups=Y_GROUPS)
    term = mix(values, panel, Z)
    term = lax.all_to_all(term, "head", 0, 0, tiled=True, axis_index_groups=Z_GROUPS)
    return jnp.sum(term.astype(F32), axis=0).astype(BF16)


def solution(mesh):
    in_specs = (
        P("dp", None),
        P("dp", "head"),
        P("dp", "head"),
        P("head", None, None),
        P("head", None, None),
        P("head", "dp", None),
        P(("dp", "head"), None, None),
        P(("dp", "head"), None, None),
        P(("dp", "head"), None),
        P(("dp", "head"), None),
        P("dp"),
        P(("dp", "head"), None),
    )
    out_specs = P("dp", "head")
    return jax.shard_map(body, mesh=mesh, in_specs=in_specs, out_specs=out_specs, check_vma=False)
```

```python
import math

import jax
import jax.numpy as jnp
from jax import lax
from jax.experimental import pallas as pl
from jax.experimental.pallas import tpu as pltpu
from jax.sharding import PartitionSpec as P

GROUP = 4
CHUNKS = 8
NOPE = 128
Y = 4
Z = 8
Z_GROUPS = [[y * Z + z for z in range(Z)] for y in range(Y)]
Y_GROUPS = [[y * Z + z for y in range(Y)] for z in range(Z)]
F32 = jnp.float32
BF16 = jnp.bfloat16
WHOLE = pl.BlockSpec(memory_space=pltpu.VMEM)
SCALARS = pl.BlockSpec(memory_space=pltpu.SMEM)
IN_HBM = pl.BlockSpec(memory_space=pltpu.HBM)


def dot(a, b):
    return jnp.dot(a, b, preferred_element_type=F32)


def in_hbm(x):
    return pltpu.with_memory_space_constraint(x, pltpu.HBM)


def params(mib):
    return pltpu.CompilerParams(vmem_limit_bytes=mib * 1024 * 1024)


def prepare_kernel(nope_hbm, rope_hbm, weights_hbm, both_ref, cut_ref, sem):
    width = nope_hbm.shape[1]
    columns = cut_ref.shape[2]
    copies = [
        pltpu.make_async_copy(nope_hbm, both_ref.at[:, :width], sem.at[0]),
        pltpu.make_async_copy(rope_hbm, both_ref.at[:, width:], sem.at[1]),
    ]
    for y in range(Y):
        source = weights_hbm.at[:, pl.ds(y * columns, columns)]
        copies.append(pltpu.make_async_copy(source, cut_ref.at[y], sem.at[2 + y]))
    for copy in copies:
        copy.start()
    for copy in copies:
        copy.wait()


def prepare(w_qnope, w_qrope, weights):
    depth = w_qnope.shape[0]
    return pl.pallas_call(
        prepare_kernel,
        out_shape=(
            jax.ShapeDtypeStruct((depth, w_qnope.shape[1] + w_qrope.shape[1]), BF16),
            jax.ShapeDtypeStruct((Y, weights.shape[0], weights.shape[1] // Y), BF16),
        ),
        in_specs=[IN_HBM] * 3,
        out_specs=(WHOLE, WHOLE),
        scratch_shapes=[pltpu.SemaphoreType.DMA((2 + Y,))],
        compiler_params=params(8),
        name="prepare",
    )(*[in_hbm(a) for a in (w_qnope, w_qrope, weights)])


def one_hot(rows, columns, place, keep=None):
    a = lax.broadcasted_iota(jnp.int32, (rows, columns), 0)
    b = lax.broadcasted_iota(jnp.int32, (rows, columns), 1)
    hit = place(a) == b
    if keep is not None:
        hit = hit & keep(a)
    return hit.astype(F32).astype(BF16)


def project_kernel(
    latent_ref, weights_hbm, uk_ref, cos_ref, sin_ref, out_ref, held_ref, sem
):
    heads, nope_dim, width = uk_ref.shape
    rows = latent_ref.shape[0]
    steps, depth, _ = held_ref.shape
    copies = [
        pltpu.make_async_copy(weights_hbm.at[pl.ds(d * depth, depth)], held_ref.at[d], sem.at[d])
        for d in range(steps)
    ]
    for copy in copies:
        copy.start()
    both = None
    for d in range(steps):
        copies[d].wait()
        term = dot(latent_ref[:, d * depth : (d + 1) * depth], held_ref[d])
        both = term if both is None else both + term
    query = both[:, : heads * nope_dim].astype(BF16)
    turned = both[:, heads * nope_dim :]
    lanes = turned.shape[1]
    rope_dim = lanes // heads
    lane = lax.broadcasted_iota(jnp.int32, turned.shape, 1)
    half = rope_dim // 2
    swapped = jnp.where(
        lane % rope_dim < half,
        pltpu.roll(turned, lanes - half, 1),
        pltpu.roll(turned, half, 1),
    )
    rotated = (turned * cos_ref[...] + swapped * sin_ref[...]).astype(BF16)
    blank = jnp.zeros((rows, out_ref.shape[1] - width - rope_dim), BF16)
    total = None
    for j in range(heads):
        part = dot(query[:, j * nope_dim : (j + 1) * nope_dim], uk_ref[j]).astype(BF16)
        part = jnp.concatenate([part, rotated[:, j * rope_dim : (j + 1) * rope_dim], blank], axis=1)
        place = one_hot(
            rows * heads, rows, lambda i: i // heads, lambda i, j=j: i % heads == j
        )
        term = dot(place, part)
        total = term if total is None else total + term
    out_ref[...] = total.astype(BF16)


def project(latent, weights, w_uk, cos, sin, parts):
    heads, _, width = w_uk.shape
    rows = latent.shape[0]
    full = width + 128 * pl.cdiv(cos.shape[1] // heads, 128)
    return pl.pallas_call(
        project_kernel,
        out_shape=jax.ShapeDtypeStruct((rows * heads, full), BF16),
        in_specs=[WHOLE, IN_HBM] + [WHOLE] * 3,
        out_specs=WHOLE,
        scratch_shapes=[
            pltpu.VMEM((parts, weights.shape[0] // parts, weights.shape[1]), BF16),
            pltpu.SemaphoreType.DMA((parts,)),
        ],
        compiler_params=params(16),
        name="project",
    )(latent, in_hbm(weights), w_uk, cos, sin)


def attend_kernel(
    length_ref, table_ref, query_ref, new_ref, new_rope_ref, latent_hbm, rope_ref, out_ref,
    scores_ref, held_ref, high_ref, absorbed_ref, rotary_ref, row_ref, slot_ref, sem,
):
    own, slots = table_ref.shape
    pool, page, width = held_ref.shape
    rope_dim = rope_ref.shape[1]
    rows = query_ref.shape[0]
    all_heads = rows // own
    heads = out_ref.shape[1] // width
    sources = all_heads // heads
    factor = math.log2(math.e) / (NOPE + rope_dim) ** 0.5
    share = pool // CHUNKS
    copies = []
    for c in range(CHUNKS):
        span = pl.ds(c * share, share)
        copies.append(pltpu.make_async_copy(latent_hbm.at[span], held_ref.at[span], sem.at[c]))
    for copy in copies:
        copy.start()
    for r in range(own):
        for i in range(slots):
            index = table_ref[r, i]
            row_ref[index] = r
            slot_ref[index] = i
    def sorted_place(i):
        return (i % all_heads) // heads * (own * heads) + i // all_heads * heads + i % heads

    ordered = dot(one_hot(rows, rows, sorted_place), query_ref[...]).astype(BF16)
    new_scores = []
    for r in range(own):
        q_abs = ordered[r * all_heads : (r + 1) * all_heads, :width]
        q_rot = ordered[r * all_heads : (r + 1) * all_heads, width : width + rope_dim]
        absorbed_ref[r] = q_abs
        rotary_ref[r] = q_rot
        new_rope = new_rope_ref[r : r + 1, :].astype(F32)
        score_new = jnp.sum(
            q_abs.astype(F32) * new_ref[r : r + 1, :].astype(F32), axis=1, keepdims=True
        )
        score_new += jnp.sum(q_rot.astype(F32) * new_rope, axis=1, keepdims=True)
        new_scores.append(score_new * factor)
    high_ref[...] = jnp.full(high_ref.shape, -jnp.inf, F32)
    for c in range(CHUNKS):
        copies[c].wait()
        for g in range(c * share, (c + 1) * share):
            r, i = row_ref[g], slot_ref[g]
            scores = lax.dot_general(
                absorbed_ref[r], held_ref[g], (((1,), (1,)), ((), ())), preferred_element_type=F32
            )
            scores = (scores + dot(rotary_ref[r], rope_ref[g])) * factor
            position = i * page + lax.broadcasted_iota(jnp.int32, scores.shape, 1)
            scores = jnp.where(position < length_ref[r], scores, -jnp.inf)
            scores_ref[r, i] = scores
            high_ref[r] = jnp.maximum(high_ref[r], scores)
    done = []
    for r in range(own):
        score_new = new_scores[r]
        top = jnp.maximum(score_new, jnp.max(high_ref[r], axis=1, keepdims=True))
        weight_new = jnp.exp2(score_new - top)
        total = None
        for i in range(slots):
            weights = jnp.exp2(scores_ref[r, i] - top)
            scores_ref[r, i] = weights
            total = weights if total is None else total + weights
        inverse = 1.0 / (jnp.sum(total, axis=1, keepdims=True) + weight_new)
        new = new_ref[r : r + 1, :].astype(F32)
        summed = (weight_new * inverse).astype(BF16).astype(F32) * new
        for i in range(0, slots, GROUP):
            group = range(i, i + GROUP)
            probs = jnp.concatenate(
                [(scores_ref[r, k] * inverse).astype(BF16) for k in group], axis=1
            )
            latents = jnp.concatenate([held_ref[table_ref[r, k]] for k in group], axis=0)
            summed += dot(probs, latents)
        done.append(summed.astype(BF16))
    count = sources // Y
    together = jnp.concatenate(done, axis=0)
    for j in range(heads):

        def place(i, j=j):
            source = (i // own) % Y * count + i // (own * Y)
            return i % own * all_heads + source * heads + j

        piece = dot(one_hot(sources * own, rows, place), together)
        out_ref[:, j * width : (j + 1) * width] = piece.astype(BF16)


def attend(lengths, table, query, heads, new_latent, new_rope, cache_latent, cache_rope):
    own, slots = table.shape
    pool, page, width = cache_latent.shape
    rope_dim = cache_rope.shape[1]
    rows = query.shape[0]
    all_heads = rows // own
    return pl.pallas_call(
        attend_kernel,
        out_shape=jax.ShapeDtypeStruct((rows // heads, heads * width), BF16),
        in_specs=[SCALARS, SCALARS] + [WHOLE] * 3 + [IN_HBM, WHOLE],
        out_specs=WHOLE,
        scratch_shapes=[
            pltpu.VMEM((own, slots, all_heads, page), F32),
            pltpu.VMEM(cache_latent.shape, BF16),
            pltpu.VMEM((own, all_heads, page), F32),
            pltpu.VMEM((own, all_heads, width), BF16),
            pltpu.VMEM((own, all_heads, rope_dim), BF16),
            pltpu.SMEM((pool,), jnp.int32),
            pltpu.SMEM((pool,), jnp.int32),
            pltpu.SemaphoreType.DMA((CHUNKS,)),
        ],
        compiler_params=params(24),
        name="attend",
    )(lengths, table, query, new_latent, new_rope, in_hbm(cache_latent), cache_rope)


def values_kernel(parts, me_ref, attn_ref, *refs):
    uv_refs, (out_ref, sorted_ref, spread_ref) = refs[:Y], refs[Y:]
    heads, width, value_dim = uv_refs[0].shape
    per = value_dim // parts
    rows = attn_ref.shape[0]
    group = rows // Y
    own = group // Z

    def place(i):
        return (i % group) // own * (Y * own) + (i // group) * own + i % own

    ordered = dot(one_hot(rows, rows, place), attn_ref[...]).astype(BF16)
    for y in range(Y):
        sorted_ref[y] = ordered[y * group : (y + 1) * group]
    columns = heads * value_dim
    source = lax.broadcasted_iota(jnp.int32, (columns, columns), 0)
    column = lax.broadcasted_iota(jnp.int32, (columns, columns), 1)
    inner = source % value_dim
    target = (inner // per) * (heads * per) + (source // value_dim) * per + inner % per
    move = (column == target).astype(F32).astype(BF16)
    for k in range(Y):
        y = lax.rem(me_ref[0] + (Y - k), Y)
        rows_y = sorted_ref[y]
        value = jnp.concatenate(
            [
                dot(rows_y[:, j * width : (j + 1) * width], uv_refs[k][j]).astype(BF16)
                for j in range(heads)
            ],
            axis=1,
        )
        spread_ref[y] = dot(value, move).astype(BF16)
    share = heads * per
    for y in range(Y):
        for d in range(parts):
            start = (d * Y + y) * share
            out_ref[:, start : start + share] = spread_ref[y, :, d * share : (d + 1) * share]


def project_values(me, attn, pieces, parts):
    heads, _, value_dim = pieces[0].shape
    rows = attn.shape[0]
    group = rows // Y

    def kernel(*refs):
        values_kernel(parts, *refs)

    return pl.pallas_call(
        kernel,
        out_shape=jax.ShapeDtypeStruct((group, Y * heads * value_dim), BF16),
        in_specs=[SCALARS] + [WHOLE] * (1 + Y),
        out_specs=WHOLE,
        scratch_shapes=[
            pltpu.VMEM((Y, group, attn.shape[1]), BF16),
            pltpu.VMEM((Y, group, heads * value_dim), BF16),
        ],
        compiler_params=params(16),
        name="values",
    )(me, attn, *pieces)


def mix_kernel(values_ref, weights_ref, out_ref, held_ref, sem):
    steps, sources, per, columns = weights_ref.shape
    depth = sources * per
    copies = [
        pltpu.make_async_copy(weights_ref.at[d], held_ref.at[d], sem.at[d]) for d in range(steps)
    ]
    for copy in copies:
        copy.start()
    total = None
    for d in range(steps):
        copies[d].wait()
        block = held_ref[d].reshape(depth, columns)
        term = dot(values_ref[:, d * depth : (d + 1) * depth], block)
        total = term if total is None else total + term
    parts, _, width = out_ref.shape
    for z in range(parts):
        out_ref[z] = total[:, z * width : (z + 1) * width].astype(BF16)


def mix(values, weights, parts):
    rows = values.shape[0]
    steps, _, _, columns = weights.shape
    return pl.pallas_call(
        mix_kernel,
        out_shape=jax.ShapeDtypeStruct((parts, rows, columns // parts), BF16),
        in_specs=[WHOLE, IN_HBM],
        out_specs=WHOLE,
        scratch_shapes=[
            pltpu.VMEM(weights.shape, BF16),
            pltpu.SemaphoreType.DMA((steps,)),
        ],
        compiler_params=params(20),
        name="mix",
    )(values, in_hbm(weights))


def finish_kernel(terms_ref, out_ref):
    total = terms_ref[0].astype(F32)
    for z in range(1, terms_ref.shape[0]):
        total += terms_ref[z].astype(F32)
    out_ref[...] = total.astype(BF16)


def finish(terms):
    return pl.pallas_call(
        finish_kernel,
        out_shape=jax.ShapeDtypeStruct(terms.shape[1:], BF16),
        in_specs=[WHOLE],
        out_specs=WHOLE,
        compiler_params=params(8),
        name="finish",
    )(terms)


def shift_y(x, along):
    pairs = [(y * Z + z, (y + along) % Y * Z + z) for y in range(Y) for z in range(Z)]
    return lax.ppermute(x, "head", pairs)


def angles(lengths, rope_dim, heads):
    half = rope_dim // 2
    freq = 10000.0 ** (-2.0 * jnp.arange(half, dtype=F32) / (2 * half))
    angle = lengths.astype(F32)[:, None] * freq
    cos, sin = jnp.cos(angle), jnp.sin(angle)
    cos = jnp.tile(cos, (1, 2 * heads))
    sin = jnp.tile(jnp.concatenate([-sin, sin], axis=1), (1, heads))
    return cos, sin


def body(
    q_latent,
    w_qnope,
    w_qrope,
    w_uk,
    w_uv,
    w_out,
    cache_latent,
    cache_rope,
    new_latent,
    new_rope,
    lengths,
    page_table,
):
    rows = q_latent.shape[0]
    heads = w_uk.shape[0]
    own = page_table.shape[0]
    width_all = w_out.shape[2]
    dp_count = lax.axis_size("dp")
    sources = lax.axis_size("head")
    depth = w_out.shape[0] * w_out.shape[1]

    head = lax.axis_index("head")
    y = head // Z
    both, cuts = prepare(w_qnope, w_qrope, w_out.reshape(depth, width_all))
    weights = lax.all_gather(both, "dp", axis=0, tiled=True)
    panel = lax.all_to_all(cuts, "head", 0, 0, tiled=True, axis_index_groups=Y_GROUPS)
    panel = lax.all_gather(panel, "dp", axis=0)
    uv = [w_uv] + [shift_y(w_uv, k) for k in range(1, Y)]

    cos, sin = angles(lengths, cache_rope.shape[1], heads)
    query = project(q_latent, weights, w_uk, cos, sin, dp_count)
    query = query.reshape(sources, own * heads, query.shape[1])
    query = lax.all_to_all(query, "head", 0, 0, tiled=True).reshape(rows * heads, -1)
    own_lengths = lax.dynamic_slice_in_dim(lengths, head * own, own)
    attn = attend(
        own_lengths, page_table, query, heads, new_latent, new_rope, cache_latent, cache_rope
    )
    attn = attn.reshape(Z, Y * own, attn.shape[1])
    attn = lax.all_to_all(attn, "head", 0, 0, tiled=True, axis_index_groups=Z_GROUPS)
    values = project_values(y.reshape(1), attn.reshape(rows, -1), uv, dp_count)
    values = jnp.broadcast_to(values[None], (Y,) + values.shape)
    values = lax.all_to_all(values, "head", 0, 0, tiled=True, axis_index_groups=Y_GROUPS)
    term = mix(values.reshape(rows, -1), panel, Z)
    term = lax.all_to_all(term, "head", 0, 0, tiled=True, axis_index_groups=Z_GROUPS)
    return finish(term)


def solution(mesh):
    in_specs = (
        P("dp", None),
        P("dp", "head"),
        P("dp", "head"),
        P("head", None, None),
        P("head", None, None),
        P("head", "dp", None),
        P(("dp", "head"), None, None),
        P(("dp", "head"), None, None),
        P(("dp", "head"), None),
        P(("dp", "head"), None),
        P("dp"),
        P(("dp", "head"), None),
    )
    out_specs = P("dp", "head")
    return jax.shard_map(body, mesh=mesh, in_specs=in_specs, out_specs=out_specs, check_vma=False)
```

```python
import math

import jax
import jax.numpy as jnp
from jax import lax
from jax.experimental import pallas as pl
from jax.experimental.pallas import tpu as pltpu
from jax.sharding import PartitionSpec as P

GROUP = 4
CHUNKS = 8
NOPE = 128
Y = 4
Z = 8
Z_GROUPS = [[y * Z + z for z in range(Z)] for y in range(Y)]
Y_GROUPS = [[y * Z + z for y in range(Y)] for z in range(Z)]
F32 = jnp.float32
BF16 = jnp.bfloat16
WHOLE = pl.BlockSpec(memory_space=pltpu.VMEM)
SCALARS = pl.BlockSpec(memory_space=pltpu.SMEM)
IN_HBM = pl.BlockSpec(memory_space=pltpu.HBM)


def dot(a, b):
    return jnp.dot(a, b, preferred_element_type=F32)


def in_hbm(x):
    return pltpu.with_memory_space_constraint(x, pltpu.HBM)


def params(mib):
    return pltpu.CompilerParams(vmem_limit_bytes=mib * 1024 * 1024)


def prepare_kernel(
    place_ref, y_ref, latent_hbm, nope_hbm, rope_hbm, weights_hbm, both_ref, out_ref, *refs
):
    cut_refs, (held_ref, sem) = refs[:Y], refs[Y:]
    width = nope_hbm.shape[1]
    columns = cut_refs[0].shape[1]
    copies = [
        pltpu.make_async_copy(nope_hbm, both_ref.at[:, :width], sem.at[0]),
        pltpu.make_async_copy(rope_hbm, both_ref.at[:, width:], sem.at[1]),
        pltpu.make_async_copy(latent_hbm, held_ref, sem.at[2]),
    ]
    for k in range(Y):
        start = pl.multiple_of(lax.rem(y_ref[0] + k, Y) * columns, 128)
        source = weights_hbm.at[:, pl.ds(start, columns)]
        copies.append(pltpu.make_async_copy(source, cut_refs[k], sem.at[3 + k]))
    for copy in copies:
        copy.start()
    copies[2].wait()
    parts, _, depth = out_ref.shape
    for d in range(parts):
        out_ref[place_ref[d]] = held_ref[:, d * depth : (d + 1) * depth]
    for copy in copies[:2] + copies[3:]:
        copy.wait()


def prepare(place, y, q_latent, w_qnope, w_qrope, weights):
    rows, width = q_latent.shape
    parts = place.shape[0]
    cut = jax.ShapeDtypeStruct((weights.shape[0], weights.shape[1] // Y), BF16)
    arrays = [in_hbm(a) for a in (q_latent, w_qnope, w_qrope, weights)]
    return pl.pallas_call(
        prepare_kernel,
        out_shape=(
            jax.ShapeDtypeStruct((w_qnope.shape[0], w_qnope.shape[1] + w_qrope.shape[1]), BF16),
            jax.ShapeDtypeStruct((parts, rows, width // parts), BF16),
        )
        + (cut,) * Y,
        in_specs=[SCALARS] * 2 + [IN_HBM] * 4,
        out_specs=(WHOLE,) * (2 + Y),
        scratch_shapes=[pltpu.VMEM(q_latent.shape, BF16), pltpu.SemaphoreType.DMA((3 + Y,))],
        compiler_params=params(8),
        name="prepare",
    )(place, y, *arrays)


def stack_kernel(y_ref, *refs):
    pieces, (out_ref, sem) = refs[:Y], refs[Y:]
    copies = []
    for k in range(Y):
        target = out_ref.at[lax.rem(y_ref[0] + (Y - k), Y)]
        copies.append(pltpu.make_async_copy(pieces[k], target, sem.at[k]))
    for copy in copies:
        copy.start()
    for copy in copies:
        copy.wait()


def stack(y, pieces):
    return pl.pallas_call(
        stack_kernel,
        out_shape=jax.ShapeDtypeStruct((Y,) + pieces[0].shape, BF16),
        in_specs=[SCALARS] + [pl.BlockSpec(memory_space=pl.ANY)] * Y,
        out_specs=IN_HBM,
        scratch_shapes=[pltpu.SemaphoreType.DMA((Y,))],
        compiler_params=params(8),
        name="stack",
    )(y, *pieces)


def one_hot(rows, columns, place, keep=None):
    a = lax.broadcasted_iota(jnp.int32, (rows, columns), 0)
    b = lax.broadcasted_iota(jnp.int32, (rows, columns), 1)
    hit = place(a) == b
    if keep is not None:
        hit = hit & keep(a)
    return hit.astype(F32).astype(BF16)


def project_kernel(pieces, latent_ref, *refs):
    piece_refs = refs[:pieces]
    uk_hbm, cos_ref, sin_ref, out_ref, uk_ref, sem = refs[pieces:]
    heads, nope_dim, width = uk_ref.shape
    rows = latent_ref.shape[1]
    copy = pltpu.make_async_copy(uk_hbm, uk_ref, sem)
    copy.start()
    both = None
    for i in range(pieces):
        term = dot(latent_ref[i], piece_refs[i][...])
        both = term if both is None else both + term
    query = both[:, : heads * nope_dim].astype(BF16)
    turned = both[:, heads * nope_dim :]
    lanes = turned.shape[1]
    rope_dim = lanes // heads
    lane = lax.broadcasted_iota(jnp.int32, turned.shape, 1)
    half = rope_dim // 2
    swapped = jnp.where(
        lane % rope_dim < half,
        pltpu.roll(turned, lanes - half, 1),
        pltpu.roll(turned, half, 1),
    )
    rotated = (turned * cos_ref[...] + swapped * sin_ref[...]).astype(BF16)
    blank = jnp.zeros((rows, out_ref.shape[1] - width - rope_dim), BF16)
    copy.wait()
    total = None
    for j in range(heads):
        part = dot(query[:, j * nope_dim : (j + 1) * nope_dim], uk_ref[j]).astype(BF16)
        part = jnp.concatenate([part, rotated[:, j * rope_dim : (j + 1) * rope_dim], blank], axis=1)
        place = one_hot(
            rows * heads, rows, lambda i: i // heads, lambda i, j=j: i % heads == j
        )
        term = dot(place, part)
        total = term if total is None else total + term
    out_ref[...] = total.astype(BF16)


def project(latent, pieces, w_uk, cos, sin):
    heads, _, width = w_uk.shape
    rows = latent.shape[1]
    full = width + 128 * pl.cdiv(cos.shape[1] // heads, 128)

    def kernel(*refs):
        project_kernel(len(pieces), *refs)

    return pl.pallas_call(
        kernel,
        out_shape=jax.ShapeDtypeStruct((rows * heads, full), BF16),
        in_specs=[WHOLE] * (1 + len(pieces)) + [IN_HBM] + [WHOLE] * 2,
        out_specs=WHOLE,
        scratch_shapes=[pltpu.VMEM(w_uk.shape, BF16), pltpu.SemaphoreType.DMA(())],
        compiler_params=params(16),
        name="project",
    )(latent, *pieces, in_hbm(w_uk), cos, sin)


def attend_kernel(
    length_ref, table_ref, query_ref, new_ref, new_rope_ref, latent_hbm, rope_ref, out_ref,
    scores_ref, held_ref, high_ref, absorbed_ref, rotary_ref, row_ref, slot_ref, sem,
):
    own, slots = table_ref.shape
    pool, page, width = held_ref.shape
    rope_dim = rope_ref.shape[1]
    rows = query_ref.shape[0]
    all_heads = rows // own
    heads = out_ref.shape[1] // width
    sources = all_heads // heads
    factor = math.log2(math.e) / (NOPE + rope_dim) ** 0.5
    share = pool // CHUNKS
    copies = []
    for c in range(CHUNKS):
        span = pl.ds(c * share, share)
        copies.append(pltpu.make_async_copy(latent_hbm.at[span], held_ref.at[span], sem.at[c]))
    for copy in copies:
        copy.start()
    for r in range(own):
        for i in range(slots):
            index = table_ref[r, i]
            row_ref[index] = r
            slot_ref[index] = i
    def sorted_place(i):
        return (i % all_heads) // heads * (own * heads) + i // all_heads * heads + i % heads

    ordered = dot(one_hot(rows, rows, sorted_place), query_ref[...]).astype(BF16)
    new_scores = []
    for r in range(own):
        q_abs = ordered[r * all_heads : (r + 1) * all_heads, :width]
        q_rot = ordered[r * all_heads : (r + 1) * all_heads, width : width + rope_dim]
        absorbed_ref[r] = q_abs
        rotary_ref[r] = q_rot
        new_rope = new_rope_ref[r : r + 1, :].astype(F32)
        score_new = jnp.sum(
            q_abs.astype(F32) * new_ref[r : r + 1, :].astype(F32), axis=1, keepdims=True
        )
        score_new += jnp.sum(q_rot.astype(F32) * new_rope, axis=1, keepdims=True)
        new_scores.append(score_new * factor)
    high_ref[...] = jnp.full(high_ref.shape, -jnp.inf, F32)
    for c in range(CHUNKS):
        copies[c].wait()
        for g in range(c * share, (c + 1) * share):
            r, i = row_ref[g], slot_ref[g]
            scores = lax.dot_general(
                absorbed_ref[r], held_ref[g], (((1,), (1,)), ((), ())), preferred_element_type=F32
            )
            scores = (scores + dot(rotary_ref[r], rope_ref[g])) * factor
            position = i * page + lax.broadcasted_iota(jnp.int32, scores.shape, 1)
            scores = jnp.where(position < length_ref[r], scores, -jnp.inf)
            scores_ref[r, i] = scores
            high_ref[r] = jnp.maximum(high_ref[r], scores)
    done = []
    for r in range(own):
        score_new = new_scores[r]
        top = jnp.maximum(score_new, jnp.max(high_ref[r], axis=1, keepdims=True))
        weight_new = jnp.exp2(score_new - top)
        total = None
        for i in range(slots):
            weights = jnp.exp2(scores_ref[r, i] - top)
            scores_ref[r, i] = weights
            total = weights if total is None else total + weights
        inverse = 1.0 / (jnp.sum(total, axis=1, keepdims=True) + weight_new)
        new = new_ref[r : r + 1, :].astype(F32)
        summed = (weight_new * inverse).astype(BF16).astype(F32) * new
        for i in range(0, slots, GROUP):
            group = range(i, i + GROUP)
            probs = jnp.concatenate(
                [(scores_ref[r, k] * inverse).astype(BF16) for k in group], axis=1
            )
            latents = jnp.concatenate([held_ref[table_ref[r, k]] for k in group], axis=0)
            summed += dot(probs, latents)
        done.append(summed.astype(BF16))
    count = sources // Y
    together = jnp.concatenate(done, axis=0)
    for j in range(heads):

        def place(i, j=j):
            source = (i // own) % Y * count + i // (own * Y)
            return i % own * all_heads + source * heads + j

        piece = dot(one_hot(sources * own, rows, place), together)
        out_ref[:, j * width : (j + 1) * width] = piece.astype(BF16)


def attend(lengths, table, query, heads, new_latent, new_rope, cache_latent, cache_rope):
    own, slots = table.shape
    pool, page, width = cache_latent.shape
    rope_dim = cache_rope.shape[1]
    rows = query.shape[0]
    all_heads = rows // own
    return pl.pallas_call(
        attend_kernel,
        out_shape=jax.ShapeDtypeStruct((rows // heads, heads * width), BF16),
        in_specs=[SCALARS, SCALARS] + [WHOLE] * 3 + [IN_HBM, WHOLE],
        out_specs=WHOLE,
        scratch_shapes=[
            pltpu.VMEM((own, slots, all_heads, page), F32),
            pltpu.VMEM(cache_latent.shape, BF16),
            pltpu.VMEM((own, all_heads, page), F32),
            pltpu.VMEM((own, all_heads, width), BF16),
            pltpu.VMEM((own, all_heads, rope_dim), BF16),
            pltpu.SMEM((pool,), jnp.int32),
            pltpu.SMEM((pool,), jnp.int32),
            pltpu.SemaphoreType.DMA((CHUNKS,)),
        ],
        compiler_params=params(24),
        name="attend",
    )(lengths, table, query, new_latent, new_rope, in_hbm(cache_latent), cache_rope)


def values_kernel(parts, me_ref, attn_ref, *refs):
    uv_hbms, (out_ref, sorted_ref, spread_ref, uv_refs, sem) = refs[:Y], refs[Y:]
    copies = [pltpu.make_async_copy(uv_hbms[k], uv_refs.at[k], sem.at[k]) for k in range(Y)]
    for copy in copies:
        copy.start()
    heads, width, value_dim = uv_hbms[0].shape
    per = value_dim // parts
    rows = attn_ref.shape[0]
    group = rows // Y
    own = group // Z

    def place(i):
        return (i % group) // own * (Y * own) + (i // group) * own + i % own

    ordered = dot(one_hot(rows, rows, place), attn_ref[...]).astype(BF16)
    for y in range(Y):
        sorted_ref[y] = ordered[y * group : (y + 1) * group]
    columns = heads * value_dim
    source = lax.broadcasted_iota(jnp.int32, (columns, columns), 0)
    column = lax.broadcasted_iota(jnp.int32, (columns, columns), 1)
    inner = source % value_dim
    target = (inner // per) * (heads * per) + (source // value_dim) * per + inner % per
    move = (column == target).astype(F32).astype(BF16)
    for k in range(Y):
        y = lax.rem(me_ref[0] + (Y - k), Y)
        rows_y = sorted_ref[y]
        copies[k].wait()
        value = jnp.concatenate(
            [
                dot(rows_y[:, j * width : (j + 1) * width], uv_refs[k, j]).astype(BF16)
                for j in range(heads)
            ],
            axis=1,
        )
        spread_ref[y] = dot(value, move).astype(BF16)
    share = heads * per
    for y in range(Y):
        for d in range(parts):
            start = (d * Y + y) * share
            out_ref[:, start : start + share] = spread_ref[y, :, d * share : (d + 1) * share]


def project_values(me, attn, pieces, parts):
    heads, _, value_dim = pieces[0].shape
    rows = attn.shape[0]
    group = rows // Y

    def kernel(*refs):
        values_kernel(parts, *refs)

    return pl.pallas_call(
        kernel,
        out_shape=jax.ShapeDtypeStruct((group, Y * heads * value_dim), BF16),
        in_specs=[SCALARS, WHOLE] + [IN_HBM] * Y,
        out_specs=WHOLE,
        scratch_shapes=[
            pltpu.VMEM((Y, group, attn.shape[1]), BF16),
            pltpu.VMEM((Y, group, heads * value_dim), BF16),
            pltpu.VMEM((Y,) + pieces[0].shape, BF16),
            pltpu.SemaphoreType.DMA((Y,)),
        ],
        compiler_params=params(16),
        name="values",
    )(me, attn, *[in_hbm(piece) for piece in pieces])


def mix_kernel(values_ref, weights_ref, out_ref, held_ref, sem):
    steps, sources, per, columns = weights_ref.shape
    depth = sources * per
    copies = [
        pltpu.make_async_copy(weights_ref.at[d], held_ref.at[d], sem.at[d]) for d in range(steps)
    ]
    for copy in copies:
        copy.start()
    total = None
    for d in range(steps):
        copies[d].wait()
        block = held_ref[d].reshape(depth, columns)
        term = dot(values_ref[:, d * depth : (d + 1) * depth], block)
        total = term if total is None else total + term
    parts, _, width = out_ref.shape
    for z in range(parts):
        out_ref[z] = total[:, z * width : (z + 1) * width].astype(BF16)


def mix(values, weights, parts):
    rows = values.shape[0]
    steps, _, _, columns = weights.shape
    return pl.pallas_call(
        mix_kernel,
        out_shape=jax.ShapeDtypeStruct((parts, rows, columns // parts), BF16),
        in_specs=[WHOLE, IN_HBM],
        out_specs=WHOLE,
        scratch_shapes=[
            pltpu.VMEM(weights.shape, BF16),
            pltpu.SemaphoreType.DMA((steps,)),
        ],
        compiler_params=params(20),
        name="mix",
    )(values, in_hbm(weights))


def finish_kernel(terms_ref, out_ref):
    total = terms_ref[0].astype(F32)
    for z in range(1, terms_ref.shape[0]):
        total += terms_ref[z].astype(F32)
    out_ref[...] = total.astype(BF16)


def finish(terms):
    return pl.pallas_call(
        finish_kernel,
        out_shape=jax.ShapeDtypeStruct(terms.shape[1:], BF16),
        in_specs=[WHOLE],
        out_specs=WHOLE,
        compiler_params=params(8),
        name="finish",
    )(terms)


def shift_dp(x, along, across):
    chips = lax.axis_size("dp") // 2
    pairs = [
        (p * 2 + c, (p + along * (1 - 2 * c)) % chips * 2 + (c ^ across))
        for p in range(chips)
        for c in range(2)
    ]
    return lax.ppermute(x, "dp", pairs)


def shift_y(x, along):
    pairs = [(y * Z + z, (y + along) % Y * Z + z) for y in range(Y) for z in range(Z)]
    return lax.ppermute(x, "head", pairs)


def piece_places():
    me = lax.axis_index("dp")
    chips = lax.axis_size("dp") // 2
    chip, core = me // 2, me % 2
    sign = 1 - 2 * core
    other = lax.rem(core + 1, 2)
    steps = [0, -1, 1, 2]
    origins = [lax.rem(chip + sign * step + chips, chips) * 2 + core for step in steps]
    origins += [lax.rem(chip - sign * step + 2 * chips, chips) * 2 + other for step in steps]
    origins = jnp.stack(origins)
    parts = jnp.arange(2 * chips)
    return jnp.sum(
        jnp.where(origins[None, :] == parts[:, None], parts[None, :], 0), axis=1
    ).astype(jnp.int32)


def angles(lengths, rope_dim, heads):
    half = rope_dim // 2
    freq = 10000.0 ** (-2.0 * jnp.arange(half, dtype=F32) / (2 * half))
    angle = lengths.astype(F32)[:, None] * freq
    cos, sin = jnp.cos(angle), jnp.sin(angle)
    cos = jnp.tile(cos, (1, 2 * heads))
    sin = jnp.tile(jnp.concatenate([-sin, sin], axis=1), (1, heads))
    return cos, sin


def body(
    q_latent,
    w_qnope,
    w_qrope,
    w_uk,
    w_uv,
    w_out,
    cache_latent,
    cache_rope,
    new_latent,
    new_rope,
    lengths,
    page_table,
):
    rows = q_latent.shape[0]
    heads = w_uk.shape[0]
    own = page_table.shape[0]
    width_all = w_out.shape[2]
    dp_count = lax.axis_size("dp")
    sources = lax.axis_size("head")
    depth = w_out.shape[0] * w_out.shape[1]

    head = lax.axis_index("head")
    y = head // Z
    cos, sin = angles(lengths, cache_rope.shape[1], heads)
    y_scalar = y.reshape(1)
    flat = w_out.reshape(depth, width_all)
    both, latent, *cuts = prepare(piece_places(), y_scalar, q_latent, w_qnope, w_qrope, flat)
    ahead, behind = shift_dp(both, 1, 0), shift_dp(both, -1, 0)
    cuts = [cuts[0]] + [shift_y(cuts[k], k) for k in range(1, Y)]
    ahead, behind, cuts, cos, sin = lax.optimization_barrier((ahead, behind, cuts, cos, sin))
    same = [both, ahead, behind, shift_dp(ahead, 1, 0)]
    other = [shift_dp(piece, 0, 1) for piece in same[:3]] + [shift_dp(ahead, 1, 1)]
    panel = lax.all_gather(stack(y_scalar, cuts), "dp", axis=0)
    uv = [w_uv] + [shift_y(w_uv, k) for k in range(1, Y)]

    query = project(latent, same + other, w_uk, cos, sin)
    query = query.reshape(sources, own * heads, query.shape[1])
    query = lax.all_to_all(query, "head", 0, 0, tiled=True).reshape(rows * heads, -1)
    own_lengths = lax.dynamic_slice_in_dim(lengths, head * own, own)
    attn = attend(
        own_lengths, page_table, query, heads, new_latent, new_rope, cache_latent, cache_rope
    )
    attn = attn.reshape(Z, Y * own, attn.shape[1])
    attn = lax.all_to_all(attn, "head", 0, 0, tiled=True, axis_index_groups=Z_GROUPS)
    values = project_values(y_scalar, attn.reshape(rows, -1), uv, dp_count)
    values = jnp.broadcast_to(values[None], (Y,) + values.shape)
    values = lax.all_to_all(values, "head", 0, 0, tiled=True, axis_index_groups=Y_GROUPS)
    term = mix(values.reshape(rows, -1), panel, Z)
    term = lax.all_to_all(term, "head", 0, 0, tiled=True, axis_index_groups=Z_GROUPS)
    return finish(term)


def solution(mesh):
    in_specs = (
        P("dp", None),
        P("dp", "head"),
        P("dp", "head"),
        P("head", None, None),
        P("head", None, None),
        P("head", "dp", None),
        P(("dp", "head"), None, None),
        P(("dp", "head"), None, None),
        P(("dp", "head"), None),
        P(("dp", "head"), None),
        P("dp"),
        P(("dp", "head"), None),
    )
    out_specs = P("dp", "head")
    return jax.shard_map(body, mesh=mesh, in_specs=in_specs, out_specs=out_specs, check_vma=False)
```

```python
import math

import jax
import jax.numpy as jnp
from jax import lax
from jax.experimental import pallas as pl
from jax.experimental.pallas import tpu as pltpu
from jax.sharding import PartitionSpec as P

GROUP = 4
CHUNKS = 8
NOPE = 128
Y = 4
Z = 8
Z_GROUPS = [[y * Z + z for z in range(Z)] for y in range(Y)]
Y_GROUPS = [[y * Z + z for y in range(Y)] for z in range(Z)]
F32 = jnp.float32
BF16 = jnp.bfloat16
WHOLE = pl.BlockSpec(memory_space=pltpu.VMEM)
SCALARS = pl.BlockSpec(memory_space=pltpu.SMEM)
IN_HBM = pl.BlockSpec(memory_space=pltpu.HBM)


def dot(a, b):
    return jnp.dot(a, b, preferred_element_type=F32)


def in_hbm(x):
    return pltpu.with_memory_space_constraint(x, pltpu.HBM)


def params(mib):
    return pltpu.CompilerParams(vmem_limit_bytes=mib * 1024 * 1024)


def prepare_kernel(y_ref, nope_hbm, rope_hbm, weights_hbm, both_ref, *refs):
    cut_refs, sem = refs[:Y], refs[Y]
    width = nope_hbm.shape[1]
    columns = cut_refs[0].shape[1]
    copies = [
        pltpu.make_async_copy(nope_hbm, both_ref.at[:, :width], sem.at[0]),
        pltpu.make_async_copy(rope_hbm, both_ref.at[:, width:], sem.at[1]),
    ]
    for k in range(Y):
        start = pl.multiple_of(lax.rem(y_ref[0] + k, Y) * columns, 128)
        source = weights_hbm.at[:, pl.ds(start, columns)]
        copies.append(pltpu.make_async_copy(source, cut_refs[k], sem.at[2 + k]))
    for copy in copies:
        copy.start()
    for copy in copies:
        copy.wait()


def prepare(y, w_qnope, w_qrope, weights):
    depth = w_qnope.shape[0]
    cut = jax.ShapeDtypeStruct((weights.shape[0], weights.shape[1] // Y), BF16)
    return pl.pallas_call(
        prepare_kernel,
        out_shape=(jax.ShapeDtypeStruct((depth, w_qnope.shape[1] + w_qrope.shape[1]), BF16),)
        + (cut,) * Y,
        in_specs=[SCALARS] + [IN_HBM] * 3,
        out_specs=(WHOLE,) * (1 + Y),
        scratch_shapes=[pltpu.SemaphoreType.DMA((2 + Y,))],
        compiler_params=params(8),
        name="prepare",
    )(y, *[in_hbm(a) for a in (w_qnope, w_qrope, weights)])


def stack_kernel(y_ref, *refs):
    pieces, (out_ref, sem) = refs[:Y], refs[Y:]
    copies = []
    for k in range(Y):
        target = out_ref.at[lax.rem(y_ref[0] + (Y - k), Y)]
        copies.append(pltpu.make_async_copy(pieces[k], target, sem.at[k]))
    for copy in copies:
        copy.start()
    for copy in copies:
        copy.wait()


def stack(y, pieces):
    return pl.pallas_call(
        stack_kernel,
        out_shape=jax.ShapeDtypeStruct((Y,) + pieces[0].shape, BF16),
        in_specs=[SCALARS] + [pl.BlockSpec(memory_space=pl.ANY)] * Y,
        out_specs=IN_HBM,
        scratch_shapes=[pltpu.SemaphoreType.DMA((Y,))],
        compiler_params=params(8),
        name="stack",
    )(y, *pieces)


def one_hot(rows, columns, place, keep=None):
    a = lax.broadcasted_iota(jnp.int32, (rows, columns), 0)
    b = lax.broadcasted_iota(jnp.int32, (rows, columns), 1)
    hit = place(a) == b
    if keep is not None:
        hit = hit & keep(a)
    return hit.astype(F32).astype(BF16)


def project_kernel(pieces, place_ref, latent_hbm, *refs):
    piece_refs = refs[:pieces]
    uk_hbm, cos_ref, sin_ref, out_ref, held_ref, sorted_ref, uk_ref, sem = refs[pieces:]
    heads, nope_dim, width = uk_ref.shape
    rows = latent_hbm.shape[0]
    copies = [
        pltpu.make_async_copy(latent_hbm, held_ref, sem.at[0]),
        pltpu.make_async_copy(uk_hbm, uk_ref, sem.at[1]),
    ]
    for copy in copies:
        copy.start()
    copies[0].wait()
    depth = sorted_ref.shape[2]
    for d in range(pieces):
        sorted_ref[place_ref[d]] = held_ref[:, d * depth : (d + 1) * depth]
    both = None
    for i in range(pieces):
        term = dot(sorted_ref[i], piece_refs[i][...])
        both = term if both is None else both + term
    query = both[:, : heads * nope_dim].astype(BF16)
    turned = both[:, heads * nope_dim :]
    lanes = turned.shape[1]
    rope_dim = lanes // heads
    lane = lax.broadcasted_iota(jnp.int32, turned.shape, 1)
    half = rope_dim // 2
    swapped = jnp.where(
        lane % rope_dim < half,
        pltpu.roll(turned, lanes - half, 1),
        pltpu.roll(turned, half, 1),
    )
    cos = jnp.concatenate([cos_ref[...]] * (2 * heads), axis=1)
    sin = jnp.concatenate([-sin_ref[...], sin_ref[...]] * heads, axis=1)
    rotated = (turned * cos + swapped * sin).astype(BF16)
    blank = jnp.zeros((rows, out_ref.shape[1] - width - rope_dim), BF16)
    copies[1].wait()
    total = None
    for j in range(heads):
        part = dot(query[:, j * nope_dim : (j + 1) * nope_dim], uk_ref[j]).astype(BF16)
        part = jnp.concatenate([part, rotated[:, j * rope_dim : (j + 1) * rope_dim], blank], axis=1)
        place = one_hot(
            rows * heads, rows, lambda i: i // heads, lambda i, j=j: i % heads == j
        )
        term = dot(place, part)
        total = term if total is None else total + term
    out_ref[...] = total.astype(BF16)


def project(place, latent, pieces, w_uk, cos, sin):
    heads, _, width = w_uk.shape
    rows = latent.shape[0]
    count = len(pieces)
    full = width + 128 * pl.cdiv(2 * cos.shape[1], 128)

    def kernel(*refs):
        project_kernel(count, *refs)

    return pl.pallas_call(
        kernel,
        out_shape=jax.ShapeDtypeStruct((rows * heads, full), BF16),
        in_specs=[SCALARS, IN_HBM] + [WHOLE] * count + [IN_HBM] + [WHOLE] * 2,
        out_specs=WHOLE,
        scratch_shapes=[
            pltpu.VMEM(latent.shape, BF16),
            pltpu.VMEM((count, rows, latent.shape[1] // count), BF16),
            pltpu.VMEM(w_uk.shape, BF16),
            pltpu.SemaphoreType.DMA((2,)),
        ],
        compiler_params=params(16),
        name="project",
    )(place, in_hbm(latent), *pieces, in_hbm(w_uk), cos, sin)


def attend_kernel(
    heads,     length_ref, table_ref, query_ref, new_ref, new_rope_ref, latent_hbm, rope_ref, out_ref,
    scores_ref, held_ref, high_ref, absorbed_ref, rotary_ref, row_ref, slot_ref, sem,
):
    own, slots = table_ref.shape
    pool, page, width = held_ref.shape
    rope_dim = rope_ref.shape[1]
    rows = query_ref.shape[0]
    all_heads = rows // own
    factor = math.log2(math.e) / (NOPE + rope_dim) ** 0.5
    share = pool // CHUNKS
    copies = []
    for c in range(CHUNKS):
        span = pl.ds(c * share, share)
        copies.append(pltpu.make_async_copy(latent_hbm.at[span], held_ref.at[span], sem.at[c]))
    for copy in copies:
        copy.start()
    for r in range(own):
        for i in range(slots):
            index = table_ref[r, i]
            row_ref[index] = r
            slot_ref[index] = i
    def sorted_place(i):
        return (i % all_heads) // heads * (own * heads) + i // all_heads * heads + i % heads

    ordered = dot(one_hot(rows, rows, sorted_place), query_ref[...]).astype(BF16)
    new_scores = []
    for r in range(own):
        q_abs = ordered[r * all_heads : (r + 1) * all_heads, :width]
        q_rot = ordered[r * all_heads : (r + 1) * all_heads, width : width + rope_dim]
        absorbed_ref[r] = q_abs
        rotary_ref[r] = q_rot
        new_rope = new_rope_ref[r : r + 1, :].astype(F32)
        score_new = jnp.sum(
            q_abs.astype(F32) * new_ref[r : r + 1, :].astype(F32), axis=1, keepdims=True
        )
        score_new += jnp.sum(q_rot.astype(F32) * new_rope, axis=1, keepdims=True)
        new_scores.append(score_new * factor)
    high_ref[...] = jnp.full(high_ref.shape, -jnp.inf, F32)
    for c in range(CHUNKS):
        copies[c].wait()
        for g in range(c * share, (c + 1) * share):
            r, i = row_ref[g], slot_ref[g]
            scores = lax.dot_general(
                absorbed_ref[r], held_ref[g], (((1,), (1,)), ((), ())), preferred_element_type=F32
            )
            scores = (scores + dot(rotary_ref[r], rope_ref[g])) * factor
            position = i * page + lax.broadcasted_iota(jnp.int32, scores.shape, 1)
            scores = jnp.where(position < length_ref[r], scores, -jnp.inf)
            scores_ref[r, i] = scores
            high_ref[r] = jnp.maximum(high_ref[r], scores)
    done = []
    for r in range(own):
        score_new = new_scores[r]
        top = jnp.maximum(score_new, jnp.max(high_ref[r], axis=1, keepdims=True))
        weight_new = jnp.exp2(score_new - top)
        total = None
        for i in range(slots):
            weights = jnp.exp2(scores_ref[r, i] - top)
            scores_ref[r, i] = weights
            total = weights if total is None else total + weights
        inverse = 1.0 / (jnp.sum(total, axis=1, keepdims=True) + weight_new)
        new = new_ref[r : r + 1, :].astype(F32)
        summed = (weight_new * inverse).astype(BF16).astype(F32) * new
        for i in range(0, slots, GROUP):
            group = range(i, i + GROUP)
            probs = jnp.concatenate(
                [(scores_ref[r, k] * inverse).astype(BF16) for k in group], axis=1
            )
            latents = jnp.concatenate([held_ref[table_ref[r, k]] for k in group], axis=0)
            summed += dot(probs, latents)
        done.append(summed.astype(BF16))
    def place(i):
        row = i % (own * heads) // heads
        return row * all_heads + i // (own * heads) * heads + i % heads

    out_ref[...] = dot(one_hot(rows, rows, place), jnp.concatenate(done, axis=0)).astype(BF16)


def attend(lengths, table, query, heads, new_latent, new_rope, cache_latent, cache_rope):
    own, slots = table.shape
    pool, page, width = cache_latent.shape
    rope_dim = cache_rope.shape[1]
    rows = query.shape[0]
    all_heads = rows // own

    def kernel(*refs):
        attend_kernel(heads, *refs)

    return pl.pallas_call(
        kernel,
        out_shape=jax.ShapeDtypeStruct((rows, width), BF16),
        in_specs=[SCALARS, SCALARS] + [WHOLE] * 3 + [IN_HBM, WHOLE],
        out_specs=WHOLE,
        scratch_shapes=[
            pltpu.VMEM((own, slots, all_heads, page), F32),
            pltpu.VMEM(cache_latent.shape, BF16),
            pltpu.VMEM((own, all_heads, page), F32),
            pltpu.VMEM((own, all_heads, width), BF16),
            pltpu.VMEM((own, all_heads, rope_dim), BF16),
            pltpu.SMEM((pool,), jnp.int32),
            pltpu.SMEM((pool,), jnp.int32),
            pltpu.SemaphoreType.DMA((CHUNKS,)),
        ],
        compiler_params=params(24),
        name="attend",
    )(lengths, table, query, new_latent, new_rope, in_hbm(cache_latent), cache_rope)


def values_kernel(parts, attn_ref, uv_hbm, out_ref, uv_ref, sem):
    copy = pltpu.make_async_copy(uv_hbm, uv_ref, sem)
    copy.start()
    heads, width, value_dim = uv_ref.shape
    per = value_dim // parts
    count = attn_ref.shape[0]
    rows = count // heads
    place = one_hot(count, count, lambda i: i % rows * heads + i // rows)
    ordered = dot(place, attn_ref[...]).astype(BF16)
    columns = heads * value_dim
    source = lax.broadcasted_iota(jnp.int32, (columns, columns), 0)
    column = lax.broadcasted_iota(jnp.int32, (columns, columns), 1)
    inner = source % value_dim
    target = (inner // per) * (heads * per) + (source // value_dim) * per + inner % per
    move = (column == target).astype(F32).astype(BF16)
    copy.wait()
    value = jnp.concatenate(
        [dot(ordered[j * rows : (j + 1) * rows], uv_ref[j]).astype(BF16) for j in range(heads)],
        axis=1,
    )
    out_ref[...] = dot(value, move).astype(BF16)


def project_values(attn, w_uv, parts):
    heads, _, value_dim = w_uv.shape

    def kernel(*refs):
        values_kernel(parts, *refs)

    return pl.pallas_call(
        kernel,
        out_shape=jax.ShapeDtypeStruct((attn.shape[0] // heads, heads * value_dim), BF16),
        in_specs=[WHOLE, IN_HBM],
        out_specs=WHOLE,
        scratch_shapes=[pltpu.VMEM(w_uv.shape, BF16), pltpu.SemaphoreType.DMA(())],
        compiler_params=params(16),
        name="values",
    )(attn, in_hbm(w_uv))


def mix_kernel(values_ref, weights_ref, out_ref, held_ref, sem):
    steps, sources, per, columns = weights_ref.shape
    depth = sources * per
    copies = [
        pltpu.make_async_copy(weights_ref.at[d], held_ref.at[d], sem.at[d]) for d in range(steps)
    ]
    for copy in copies:
        copy.start()
    total = None
    for d in range(steps):
        copies[d].wait()
        block = held_ref[d].reshape(depth, columns)
        part = jnp.concatenate(
            [values_ref[y, :, d * per : (d + 1) * per] for y in range(sources)], axis=1
        )
        term = dot(part, block)
        total = term if total is None else total + term
    parts, _, width = out_ref.shape
    for z in range(parts):
        out_ref[z] = total[:, z * width : (z + 1) * width].astype(BF16)


def mix(values, weights, parts):
    rows = values.shape[1]
    steps, _, _, columns = weights.shape
    return pl.pallas_call(
        mix_kernel,
        out_shape=jax.ShapeDtypeStruct((parts, rows, columns // parts), BF16),
        in_specs=[WHOLE, IN_HBM],
        out_specs=WHOLE,
        scratch_shapes=[
            pltpu.VMEM(weights.shape, BF16),
            pltpu.SemaphoreType.DMA((steps,)),
        ],
        compiler_params=params(20),
        name="mix",
    )(values, in_hbm(weights))


def finish_kernel(terms_ref, out_ref):
    total = terms_ref[0].astype(F32)
    for z in range(1, terms_ref.shape[0]):
        total += terms_ref[z].astype(F32)
    out_ref[...] = total.astype(BF16)


def finish(terms):
    return pl.pallas_call(
        finish_kernel,
        out_shape=jax.ShapeDtypeStruct(terms.shape[1:], BF16),
        in_specs=[WHOLE],
        out_specs=WHOLE,
        compiler_params=params(8),
        name="finish",
    )(terms)


def shift_dp(x, along, across):
    chips = lax.axis_size("dp") // 2
    pairs = [
        (p * 2 + c, (p + along * (1 - 2 * c)) % chips * 2 + (c ^ across))
        for p in range(chips)
        for c in range(2)
    ]
    return lax.ppermute(x, "dp", pairs)


def shift_y(x, along):
    pairs = [(y * Z + z, (y + along) % Y * Z + z) for y in range(Y) for z in range(Z)]
    return lax.ppermute(x, "head", pairs)


def piece_places():
    me = lax.axis_index("dp")
    chips = lax.axis_size("dp") // 2
    chip, core = me // 2, me % 2
    sign = 1 - 2 * core
    other = lax.rem(core + 1, 2)
    steps = [0, -1, 1, 2]
    origins = [lax.rem(chip + sign * step + chips, chips) * 2 + core for step in steps]
    origins += [lax.rem(chip - sign * step + 2 * chips, chips) * 2 + other for step in steps]
    origins = jnp.stack(origins)
    parts = jnp.arange(2 * chips)
    return jnp.sum(
        jnp.where(origins[None, :] == parts[:, None], parts[None, :], 0), axis=1
    ).astype(jnp.int32)


def angles(lengths, rope_dim):
    half = rope_dim // 2
    freq = 10000.0 ** (-2.0 * jnp.arange(half, dtype=F32) / (2 * half))
    angle = lengths.astype(F32)[:, None] * freq
    return jnp.cos(angle), jnp.sin(angle)


def body(
    q_latent,
    w_qnope,
    w_qrope,
    w_uk,
    w_uv,
    w_out,
    cache_latent,
    cache_rope,
    new_latent,
    new_rope,
    lengths,
    page_table,
):
    rows = q_latent.shape[0]
    heads = w_uk.shape[0]
    own = page_table.shape[0]
    width_all = w_out.shape[2]
    dp_count = lax.axis_size("dp")
    sources = lax.axis_size("head")
    depth = w_out.shape[0] * w_out.shape[1]

    head = lax.axis_index("head")
    y = head // Z
    cos, sin = angles(lengths, cache_rope.shape[1])
    y_scalar = y.reshape(1)
    flat = w_out.reshape(depth, width_all)
    both, *cuts = prepare(y_scalar, w_qnope, w_qrope, flat)
    ahead, behind, beside = shift_dp(both, 1, 0), shift_dp(both, -1, 0), shift_dp(both, 0, 1)
    cuts[1], cuts[3] = shift_y(cuts[1], 1), shift_y(cuts[3], 3)
    ahead, behind, beside, cuts, cos, sin = lax.optimization_barrier(
        (ahead, behind, beside, cuts, cos, sin)
    )
    far = shift_dp(ahead, 1, 0)
    ahead_beside, behind_beside = shift_dp(ahead, 0, 1), shift_dp(behind, 0, 1)
    cuts[2] = shift_y(cuts[2], 2)
    cuts, far, ahead_beside, behind_beside = lax.optimization_barrier(
        (cuts, far, ahead_beside, behind_beside)
    )
    panel = lax.all_gather(stack(y_scalar, cuts), "dp", axis=0)
    pieces = [both, ahead, behind, far]
    pieces += [beside, ahead_beside, behind_beside, shift_dp(far, 0, 1)]
    query = project(piece_places(), q_latent, pieces, w_uk, cos, sin)
    query = query.reshape(sources, own * heads, query.shape[1])
    query = lax.all_to_all(query, "head", 0, 0, tiled=True).reshape(rows * heads, -1)
    own_lengths = lax.dynamic_slice_in_dim(lengths, head * own, own)
    attn = attend(
        own_lengths, page_table, query, heads, new_latent, new_rope, cache_latent, cache_rope
    )
    attn = attn.reshape(sources, own * heads, attn.shape[1])
    attn = lax.all_to_all(attn, "head", 0, 0, tiled=True).reshape(rows * heads, -1)
    values = project_values(attn, w_uv, dp_count)
    values = jnp.broadcast_to(values[None], (Y,) + values.shape)
    values = lax.all_to_all(values, "head", 0, 0, tiled=True, axis_index_groups=Y_GROUPS)
    term = mix(values, panel, Z)
    term = lax.all_to_all(term, "head", 0, 0, tiled=True, axis_index_groups=Z_GROUPS)
    return finish(term)


def solution(mesh):
    in_specs = (
        P("dp", None),
        P("dp", "head"),
        P("dp", "head"),
        P("head", None, None),
        P("head", None, None),
        P("head", "dp", None),
        P(("dp", "head"), None, None),
        P(("dp", "head"), None, None),
        P(("dp", "head"), None),
        P(("dp", "head"), None),
        P("dp"),
        P(("dp", "head"), None),
    )
    out_specs = P("dp", "head")
    return jax.shard_map(body, mesh=mesh, in_specs=in_specs, out_specs=out_specs, check_vma=False)
```

```python
import math

import jax
import jax.numpy as jnp
from jax import lax
from jax.experimental import pallas as pl
from jax.experimental.pallas import tpu as pltpu
from jax.sharding import PartitionSpec as P

GROUP = 4
CHUNKS = 4
NOPE = 128
Y = 4
Z = 8
Z_GROUPS = [[y * Z + z for z in range(Z)] for y in range(Y)]
Y_GROUPS = [[y * Z + z for y in range(Y)] for z in range(Z)]
F32 = jnp.float32
BF16 = jnp.bfloat16
WHOLE = pl.BlockSpec(memory_space=pltpu.VMEM)
SCALARS = pl.BlockSpec(memory_space=pltpu.SMEM)
IN_HBM = pl.BlockSpec(memory_space=pltpu.HBM)


def dot(a, b):
    return jnp.dot(a, b, preferred_element_type=F32)


def in_hbm(x):
    return pltpu.with_memory_space_constraint(x, pltpu.HBM)


def params(mib):
    return pltpu.CompilerParams(vmem_limit_bytes=mib * 1024 * 1024)


def prepare_kernel(y_ref, nope_hbm, rope_hbm, weights_hbm, both_ref, *refs):
    cut_refs, sem = refs[:Y], refs[Y]
    width = nope_hbm.shape[1]
    columns = cut_refs[0].shape[1]
    copies = [
        pltpu.make_async_copy(nope_hbm, both_ref.at[:, :width], sem.at[0]),
        pltpu.make_async_copy(rope_hbm, both_ref.at[:, width:], sem.at[1]),
    ]
    for k in range(Y):
        start = pl.multiple_of(lax.rem(y_ref[0] + k, Y) * columns, 128)
        source = weights_hbm.at[:, pl.ds(start, columns)]
        copies.append(pltpu.make_async_copy(source, cut_refs[k], sem.at[2 + k]))
    for copy in copies:
        copy.start()
    for copy in copies:
        copy.wait()


def prepare(y, w_qnope, w_qrope, weights):
    depth = w_qnope.shape[0]
    cut = jax.ShapeDtypeStruct((weights.shape[0], weights.shape[1] // Y), BF16)
    return pl.pallas_call(
        prepare_kernel,
        out_shape=(jax.ShapeDtypeStruct((depth, w_qnope.shape[1] + w_qrope.shape[1]), BF16),)
        + (cut,) * Y,
        in_specs=[SCALARS] + [IN_HBM] * 3,
        out_specs=(WHOLE,) * (1 + Y),
        scratch_shapes=[pltpu.SemaphoreType.DMA((2 + Y,))],
        compiler_params=params(8),
        name="prepare",
    )(y, *[in_hbm(a) for a in (w_qnope, w_qrope, weights)])


def arrange_kernel(place_ref, latent_hbm, uk_hbm, out_ref, uk_ref, held_ref, sem):
    copies = [
        pltpu.make_async_copy(latent_hbm, held_ref, sem.at[0]),
        pltpu.make_async_copy(uk_hbm, uk_ref, sem.at[1]),
    ]
    for copy in copies:
        copy.start()
    copies[0].wait()
    parts, _, depth = out_ref.shape
    for d in range(parts):
        out_ref[place_ref[d]] = held_ref[:, d * depth : (d + 1) * depth]
    copies[1].wait()


def arrange(place, latent, w_uk):
    rows, width = latent.shape
    parts = place.shape[0]
    return pl.pallas_call(
        arrange_kernel,
        out_shape=(
            jax.ShapeDtypeStruct((parts, rows, width // parts), BF16),
            jax.ShapeDtypeStruct(w_uk.shape, BF16),
        ),
        in_specs=[SCALARS] + [IN_HBM] * 2,
        out_specs=(WHOLE, WHOLE),
        scratch_shapes=[pltpu.VMEM(latent.shape, BF16), pltpu.SemaphoreType.DMA((2,))],
        compiler_params=params(8),
        name="arrange",
    )(place, in_hbm(latent), in_hbm(w_uk))


def stack_kernel(y_ref, *refs):
    pieces, (out_ref, sem) = refs[:Y], refs[Y:]
    copies = []
    for k in range(Y):
        target = out_ref.at[lax.rem(y_ref[0] + (Y - k), Y)]
        copies.append(pltpu.make_async_copy(pieces[k], target, sem.at[k]))
    for copy in copies:
        copy.start()
    for copy in copies:
        copy.wait()


def stack(y, pieces):
    return pl.pallas_call(
        stack_kernel,
        out_shape=jax.ShapeDtypeStruct((Y,) + pieces[0].shape, BF16),
        in_specs=[SCALARS] + [pl.BlockSpec(memory_space=pl.ANY)] * Y,
        out_specs=IN_HBM,
        scratch_shapes=[pltpu.SemaphoreType.DMA((Y,))],
        compiler_params=params(8),
        name="stack",
    )(y, *pieces)


def one_hot(rows, columns, place, keep=None):
    a = lax.broadcasted_iota(jnp.int32, (rows, columns), 0)
    b = lax.broadcasted_iota(jnp.int32, (rows, columns), 1)
    hit = place(a) == b
    if keep is not None:
        hit = hit & keep(a)
    return hit.astype(F32).astype(BF16)


def project_kernel(pieces, latent_ref, *refs):
    piece_refs = refs[:pieces]
    uk_ref, cos_ref, sin_ref, out_ref = refs[pieces:]
    heads, nope_dim, width = uk_ref.shape
    rows = latent_ref.shape[1]
    both = None
    for i in range(pieces):
        term = dot(latent_ref[i], piece_refs[i][...])
        both = term if both is None else both + term
    query = both[:, : heads * nope_dim].astype(BF16)
    turned = both[:, heads * nope_dim :]
    lanes = turned.shape[1]
    rope_dim = lanes // heads
    lane = lax.broadcasted_iota(jnp.int32, turned.shape, 1)
    half = rope_dim // 2
    swapped = jnp.where(
        lane % rope_dim < half,
        pltpu.roll(turned, lanes - half, 1),
        pltpu.roll(turned, half, 1),
    )
    cos = jnp.concatenate([cos_ref[...]] * (2 * heads), axis=1)
    sin = jnp.concatenate([-sin_ref[...], sin_ref[...]] * heads, axis=1)
    rotated = (turned * cos + swapped * sin).astype(BF16)
    blank = jnp.zeros((rows, out_ref.shape[1] - width - rope_dim), BF16)
    total = None
    for j in range(heads):
        part = dot(query[:, j * nope_dim : (j + 1) * nope_dim], uk_ref[j]).astype(BF16)
        part = jnp.concatenate([part, rotated[:, j * rope_dim : (j + 1) * rope_dim], blank], axis=1)
        place = one_hot(
            rows * heads, rows, lambda i: i // heads, lambda i, j=j: i % heads == j
        )
        term = dot(place, part)
        total = term if total is None else total + term
    out_ref[...] = total.astype(BF16)


def project(latent, pieces, w_uk, cos, sin):
    heads, _, width = w_uk.shape
    rows = latent.shape[1]
    count = len(pieces)
    full = width + 128 * pl.cdiv(2 * cos.shape[1], 128)

    def kernel(*refs):
        project_kernel(count, *refs)

    return pl.pallas_call(
        kernel,
        out_shape=jax.ShapeDtypeStruct((rows * heads, full), BF16),
        in_specs=[WHOLE] * (4 + count),
        out_specs=WHOLE,
        compiler_params=params(16),
        name="project",
    )(latent, *pieces, w_uk, cos, sin)


def attend_kernel(
    heads,     length_ref, table_ref, query_ref, new_ref, new_rope_ref, latent_hbm, rope_ref, out_ref,
    scores_ref, held_ref, high_ref, absorbed_ref, rotary_ref, row_ref, slot_ref, sem,
):
    own, slots = table_ref.shape
    pool, page, width = held_ref.shape
    rope_dim = rope_ref.shape[1]
    rows = query_ref.shape[0]
    all_heads = rows // own
    factor = math.log2(math.e) / (NOPE + rope_dim) ** 0.5
    share = pool // CHUNKS
    copies = []
    for c in range(CHUNKS):
        span = pl.ds(c * share, share)
        copies.append(pltpu.make_async_copy(latent_hbm.at[span], held_ref.at[span], sem.at[c]))
    for copy in copies:
        copy.start()
    for r in range(own):
        for i in range(slots):
            index = table_ref[r, i]
            row_ref[index] = r
            slot_ref[index] = i
    def sorted_place(i):
        return (i % all_heads) // heads * (own * heads) + i // all_heads * heads + i % heads

    ordered = dot(one_hot(rows, rows, sorted_place), query_ref[...]).astype(BF16)
    new_scores = []
    for r in range(own):
        q_abs = ordered[r * all_heads : (r + 1) * all_heads, :width]
        q_rot = ordered[r * all_heads : (r + 1) * all_heads, width : width + rope_dim]
        absorbed_ref[r] = q_abs
        rotary_ref[r] = q_rot
        new_rope = new_rope_ref[r : r + 1, :].astype(F32)
        score_new = jnp.sum(
            q_abs.astype(F32) * new_ref[r : r + 1, :].astype(F32), axis=1, keepdims=True
        )
        score_new += jnp.sum(q_rot.astype(F32) * new_rope, axis=1, keepdims=True)
        new_scores.append(score_new * factor)
    high_ref[...] = jnp.full(high_ref.shape, -jnp.inf, F32)
    for c in range(CHUNKS):
        copies[c].wait()
        for g in range(c * share, (c + 1) * share):
            r, i = row_ref[g], slot_ref[g]
            scores = lax.dot_general(
                absorbed_ref[r], held_ref[g], (((1,), (1,)), ((), ())), preferred_element_type=F32
            )
            scores = (scores + dot(rotary_ref[r], rope_ref[g])) * factor
            position = i * page + lax.broadcasted_iota(jnp.int32, scores.shape, 1)
            scores = jnp.where(position < length_ref[r], scores, -jnp.inf)
            scores_ref[r, i] = scores
            high_ref[r] = jnp.maximum(high_ref[r], scores)
    done = []
    for r in range(own):
        score_new = new_scores[r]
        top = jnp.maximum(score_new, jnp.max(high_ref[r], axis=1, keepdims=True))
        weight_new = jnp.exp2(score_new - top)
        total = None
        for i in range(slots):
            weights = jnp.exp2(scores_ref[r, i] - top)
            scores_ref[r, i] = weights
            total = weights if total is None else total + weights
        inverse = 1.0 / (jnp.sum(total, axis=1, keepdims=True) + weight_new)
        new = new_ref[r : r + 1, :].astype(F32)
        summed = (weight_new * inverse).astype(BF16).astype(F32) * new
        for i in range(0, slots, GROUP):
            group = range(i, i + GROUP)
            probs = jnp.concatenate(
                [(scores_ref[r, k] * inverse).astype(BF16) for k in group], axis=1
            )
            latents = jnp.concatenate([held_ref[table_ref[r, k]] for k in group], axis=0)
            summed += dot(probs, latents)
        done.append(summed.astype(BF16))
    def place(i):
        row = i % (own * heads) // heads
        return row * all_heads + i // (own * heads) * heads + i % heads

    out_ref[...] = dot(one_hot(rows, rows, place), jnp.concatenate(done, axis=0)).astype(BF16)


def attend(lengths, table, query, heads, new_latent, new_rope, cache_latent, cache_rope):
    own, slots = table.shape
    pool, page, width = cache_latent.shape
    rope_dim = cache_rope.shape[1]
    rows = query.shape[0]
    all_heads = rows // own

    def kernel(*refs):
        attend_kernel(heads, *refs)

    return pl.pallas_call(
        kernel,
        out_shape=jax.ShapeDtypeStruct((rows, width), BF16),
        in_specs=[SCALARS, SCALARS] + [WHOLE] * 3 + [IN_HBM, WHOLE],
        out_specs=WHOLE,
        scratch_shapes=[
            pltpu.VMEM((own, slots, all_heads, page), F32),
            pltpu.VMEM(cache_latent.shape, BF16),
            pltpu.VMEM((own, all_heads, page), F32),
            pltpu.VMEM((own, all_heads, width), BF16),
            pltpu.VMEM((own, all_heads, rope_dim), BF16),
            pltpu.SMEM((pool,), jnp.int32),
            pltpu.SMEM((pool,), jnp.int32),
            pltpu.SemaphoreType.DMA((CHUNKS,)),
        ],
        compiler_params=params(24),
        name="attend",
    )(lengths, table, query, new_latent, new_rope, in_hbm(cache_latent), cache_rope)


def values_kernel(parts, attn_ref, uv_hbm, out_ref, uv_ref, sem):
    copy = pltpu.make_async_copy(uv_hbm, uv_ref, sem)
    copy.start()
    heads, width, value_dim = uv_ref.shape
    per = value_dim // parts
    count = attn_ref.shape[0]
    rows = count // heads
    place = one_hot(count, count, lambda i: i % rows * heads + i // rows)
    ordered = dot(place, attn_ref[...]).astype(BF16)
    columns = heads * value_dim
    source = lax.broadcasted_iota(jnp.int32, (columns, columns), 0)
    column = lax.broadcasted_iota(jnp.int32, (columns, columns), 1)
    inner = source % value_dim
    target = (inner // per) * (heads * per) + (source // value_dim) * per + inner % per
    move = (column == target).astype(F32).astype(BF16)
    copy.wait()
    value = jnp.concatenate(
        [dot(ordered[j * rows : (j + 1) * rows], uv_ref[j]).astype(BF16) for j in range(heads)],
        axis=1,
    )
    out_ref[...] = dot(value, move).astype(BF16)


def project_values(attn, w_uv, parts):
    heads, _, value_dim = w_uv.shape

    def kernel(*refs):
        values_kernel(parts, *refs)

    return pl.pallas_call(
        kernel,
        out_shape=jax.ShapeDtypeStruct((attn.shape[0] // heads, heads * value_dim), BF16),
        in_specs=[WHOLE, IN_HBM],
        out_specs=WHOLE,
        scratch_shapes=[pltpu.VMEM(w_uv.shape, BF16), pltpu.SemaphoreType.DMA(())],
        compiler_params=params(16),
        name="values",
    )(attn, in_hbm(w_uv))


def mix_kernel(values_ref, weights_ref, out_ref, held_ref, sem):
    steps, sources, per, columns = weights_ref.shape
    depth = sources * per
    copies = [
        pltpu.make_async_copy(weights_ref.at[d], held_ref.at[d], sem.at[d]) for d in range(steps)
    ]
    for copy in copies:
        copy.start()
    total = None
    for d in range(steps):
        copies[d].wait()
        block = held_ref[d].reshape(depth, columns)
        part = jnp.concatenate(
            [values_ref[y, :, d * per : (d + 1) * per] for y in range(sources)], axis=1
        )
        term = dot(part, block)
        total = term if total is None else total + term
    parts, _, width = out_ref.shape
    for z in range(parts):
        out_ref[z] = total[:, z * width : (z + 1) * width].astype(BF16)


def mix(values, weights, parts):
    rows = values.shape[1]
    steps, _, _, columns = weights.shape
    return pl.pallas_call(
        mix_kernel,
        out_shape=jax.ShapeDtypeStruct((parts, rows, columns // parts), BF16),
        in_specs=[WHOLE, IN_HBM],
        out_specs=WHOLE,
        scratch_shapes=[
            pltpu.VMEM(weights.shape, BF16),
            pltpu.SemaphoreType.DMA((steps,)),
        ],
        compiler_params=params(20),
        name="mix",
    )(values, in_hbm(weights))


def finish_kernel(terms_ref, out_ref):
    total = terms_ref[0].astype(F32)
    for z in range(1, terms_ref.shape[0]):
        total += terms_ref[z].astype(F32)
    out_ref[...] = total.astype(BF16)


def finish(terms):
    return pl.pallas_call(
        finish_kernel,
        out_shape=jax.ShapeDtypeStruct(terms.shape[1:], BF16),
        in_specs=[WHOLE],
        out_specs=WHOLE,
        compiler_params=params(8),
        name="finish",
    )(terms)


def shift_dp(x, along, across):
    chips = lax.axis_size("dp") // 2
    pairs = [
        (p * 2 + c, (p + along * (1 - 2 * c)) % chips * 2 + (c ^ across))
        for p in range(chips)
        for c in range(2)
    ]
    return lax.ppermute(x, "dp", pairs)


def shift_y(x, along):
    pairs = [(y * Z + z, (y + along) % Y * Z + z) for y in range(Y) for z in range(Z)]
    return lax.ppermute(x, "head", pairs)


def piece_places():
    me = lax.axis_index("dp")
    chips = lax.axis_size("dp") // 2
    chip, core = me // 2, me % 2
    sign = 1 - 2 * core
    other = lax.rem(core + 1, 2)
    origins = [lax.rem(chip + sign * step + chips, chips) * 2 + core for step in (0, -1, 1, 2)]
    origins += [lax.rem(chip - sign * step + 2 * chips, chips) * 2 + other for step in (0, -1, 1, 2)]
    origins = jnp.stack(origins)
    parts = jnp.arange(2 * chips)
    return jnp.sum(
        jnp.where(origins[None, :] == parts[:, None], parts[None, :], 0), axis=1
    ).astype(jnp.int32)


def angles(lengths, rope_dim):
    half = rope_dim // 2
    freq = 10000.0 ** (-2.0 * jnp.arange(half, dtype=F32) / (2 * half))
    angle = lengths.astype(F32)[:, None] * freq
    return jnp.cos(angle), jnp.sin(angle)


def body(
    q_latent,
    w_qnope,
    w_qrope,
    w_uk,
    w_uv,
    w_out,
    cache_latent,
    cache_rope,
    new_latent,
    new_rope,
    lengths,
    page_table,
):
    rows = q_latent.shape[0]
    heads = w_uk.shape[0]
    own = page_table.shape[0]
    width_all = w_out.shape[2]
    dp_count = lax.axis_size("dp")
    sources = lax.axis_size("head")
    depth = w_out.shape[0] * w_out.shape[1]

    head = lax.axis_index("head")
    y = head // Z
    cos, sin = angles(lengths, cache_rope.shape[1])
    y_scalar = y.reshape(1)
    flat = w_out.reshape(depth, width_all)
    both, *cuts = prepare(y_scalar, w_qnope, w_qrope, flat)
    ahead, behind, beside = shift_dp(both, 1, 0), shift_dp(both, -1, 0), shift_dp(both, 0, 1)
    cuts[2] = shift_y(cuts[2], 2)
    latent, uk = arrange(piece_places(), q_latent, w_uk)
    ahead, behind, beside, cuts, cos, sin, latent, uk = lax.optimization_barrier(
        (ahead, behind, beside, cuts, cos, sin, latent, uk)
    )
    far = shift_dp(ahead, 1, 0)
    ahead_beside, behind_beside = shift_dp(ahead, 0, 1), shift_dp(behind, 0, 1)
    cuts[1], cuts[3] = shift_y(cuts[1], 1), shift_y(cuts[3], 3)
    far, cuts, ahead_beside, behind_beside = lax.optimization_barrier(
        (far, cuts, ahead_beside, behind_beside)
    )
    pieces = [both, ahead, behind, far, beside]
    pieces += [ahead_beside, behind_beside, shift_dp(far, 0, 1)]
    cuts, pieces = lax.optimization_barrier((cuts, pieces))
    panel = lax.all_gather(stack(y_scalar, cuts), "dp", axis=0)
    query = project(latent, pieces, uk, cos, sin)
    query = query.reshape(sources, own * heads, query.shape[1])
    query = lax.all_to_all(query, "head", 0, 0, tiled=True).reshape(rows * heads, -1)
    own_lengths = lax.dynamic_slice_in_dim(lengths, head * own, own)
    attn = attend(
        own_lengths, page_table, query, heads, new_latent, new_rope, cache_latent, cache_rope
    )
    attn = attn.reshape(sources, own * heads, attn.shape[1])
    attn = lax.all_to_all(attn, "head", 0, 0, tiled=True).reshape(rows * heads, -1)
    values = project_values(attn, w_uv, dp_count)
    values = jnp.broadcast_to(values[None], (Y,) + values.shape)
    values = lax.all_to_all(values, "head", 0, 0, tiled=True, axis_index_groups=Y_GROUPS)
    term = mix(values, panel, Z)
    term = lax.all_to_all(term, "head", 0, 0, tiled=True, axis_index_groups=Z_GROUPS)
    return finish(term)


def solution(mesh):
    in_specs = (
        P("dp", None),
        P("dp", "head"),
        P("dp", "head"),
        P("head", None, None),
        P("head", None, None),
        P("head", "dp", None),
        P(("dp", "head"), None, None),
        P(("dp", "head"), None, None),
        P(("dp", "head"), None),
        P(("dp", "head"), None),
        P("dp"),
        P(("dp", "head"), None),
    )
    out_specs = P("dp", "head")
    return jax.shard_map(body, mesh=mesh, in_specs=in_specs, out_specs=out_specs, check_vma=False)
```

```python
import math

import jax
import jax.numpy as jnp
from jax import lax
from jax.experimental import pallas as pl
from jax.experimental.pallas import tpu as pltpu
from jax.sharding import PartitionSpec as P

GROUP = 4
CHUNKS = 4
NOPE = 128
Y = 4
Z = 8
Z_GROUPS = [[y * Z + z for z in range(Z)] for y in range(Y)]
Y_GROUPS = [[y * Z + z for y in range(Y)] for z in range(Z)]
F32 = jnp.float32
BF16 = jnp.bfloat16
WHOLE = pl.BlockSpec(memory_space=pltpu.VMEM)
SCALARS = pl.BlockSpec(memory_space=pltpu.SMEM)
IN_HBM = pl.BlockSpec(memory_space=pltpu.HBM)


def dot(a, b):
    return jnp.dot(a, b, preferred_element_type=F32)


def in_hbm(x):
    return pltpu.with_memory_space_constraint(x, pltpu.HBM)


def params(mib):
    return pltpu.CompilerParams(vmem_limit_bytes=mib * 1024 * 1024)


def prepare_kernel(y_ref, nope_hbm, rope_hbm, weights_hbm, both_ref, *refs):
    cut_refs, sem = refs[:Y], refs[Y]
    width = nope_hbm.shape[1]
    columns = cut_refs[0].shape[1]
    copies = [
        pltpu.make_async_copy(nope_hbm, both_ref.at[:, :width], sem.at[0]),
        pltpu.make_async_copy(rope_hbm, both_ref.at[:, width:], sem.at[1]),
    ]
    for k in range(Y):
        start = pl.multiple_of(lax.rem(y_ref[0] + k, Y) * columns, 128)
        source = weights_hbm.at[:, pl.ds(start, columns)]
        copies.append(pltpu.make_async_copy(source, cut_refs[k], sem.at[2 + k]))
    for copy in copies:
        copy.start()
    for copy in copies:
        copy.wait()


def prepare(y, w_qnope, w_qrope, weights):
    depth = w_qnope.shape[0]
    cut = pltpu.HBM((weights.shape[0], weights.shape[1] // Y), BF16)
    return pl.pallas_call(
        prepare_kernel,
        out_shape=(jax.ShapeDtypeStruct((depth, w_qnope.shape[1] + w_qrope.shape[1]), BF16),)
        + (cut,) * Y,
        in_specs=[SCALARS] + [IN_HBM] * 3,
        out_specs=(WHOLE,) + (IN_HBM,) * Y,
        scratch_shapes=[pltpu.SemaphoreType.DMA((2 + Y,))],
        compiler_params=params(8),
        name="prepare",
    )(y, *[in_hbm(a) for a in (w_qnope, w_qrope, weights)])


def arrange_kernel(place_ref, latent_hbm, out_ref, held_ref, sem):
    copy = pltpu.make_async_copy(latent_hbm, held_ref, sem)
    copy.start()
    copy.wait()
    parts, _, depth = out_ref.shape
    for d in range(parts):
        out_ref[place_ref[d]] = held_ref[:, d * depth : (d + 1) * depth]


def arrange(place, latent):
    rows, width = latent.shape
    parts = place.shape[0]
    return pl.pallas_call(
        arrange_kernel,
        out_shape=jax.ShapeDtypeStruct((parts, rows, width // parts), BF16),
        in_specs=[SCALARS, IN_HBM],
        out_specs=WHOLE,
        scratch_shapes=[pltpu.VMEM(latent.shape, BF16), pltpu.SemaphoreType.DMA(())],
        compiler_params=params(8),
        name="arrange",
    )(place, in_hbm(latent))


def stack_kernel(y_ref, *refs):
    pieces, (out_ref, sem) = refs[:Y], refs[Y:]
    copies = []
    for k in range(Y):
        target = out_ref.at[lax.rem(y_ref[0] + (Y - k), Y)]
        copies.append(pltpu.make_async_copy(pieces[k], target, sem.at[k]))
    for copy in copies:
        copy.start()
    for copy in copies:
        copy.wait()


def stack(y, pieces):
    return pl.pallas_call(
        stack_kernel,
        out_shape=jax.ShapeDtypeStruct((Y,) + pieces[0].shape, BF16),
        in_specs=[SCALARS] + [IN_HBM] * Y,
        out_specs=IN_HBM,
        scratch_shapes=[pltpu.SemaphoreType.DMA((Y,))],
        compiler_params=params(8),
        name="stack",
    )(y, *[in_hbm(piece) for piece in pieces])


def one_hot(rows, columns, place, keep=None):
    a = lax.broadcasted_iota(jnp.int32, (rows, columns), 0)
    b = lax.broadcasted_iota(jnp.int32, (rows, columns), 1)
    hit = place(a) == b
    if keep is not None:
        hit = hit & keep(a)
    return hit.astype(F32).astype(BF16)


def project_kernel(pieces, latent_ref, *refs):
    piece_refs = refs[:pieces]
    uk_hbm, cos_ref, sin_ref, out_ref, uk_ref, sem = refs[pieces:]
    heads, nope_dim, width = uk_ref.shape
    rows = latent_ref.shape[1]
    copy = pltpu.make_async_copy(uk_hbm, uk_ref, sem)
    copy.start()
    both = None
    for i in range(pieces):
        term = dot(latent_ref[i], piece_refs[i][...])
        both = term if both is None else both + term
    query = both[:, : heads * nope_dim].astype(BF16)
    turned = both[:, heads * nope_dim :]
    lanes = turned.shape[1]
    rope_dim = lanes // heads
    lane = lax.broadcasted_iota(jnp.int32, turned.shape, 1)
    half = rope_dim // 2
    swapped = jnp.where(
        lane % rope_dim < half,
        pltpu.roll(turned, lanes - half, 1),
        pltpu.roll(turned, half, 1),
    )
    cos = jnp.concatenate([cos_ref[...]] * (2 * heads), axis=1)
    sin = jnp.concatenate([-sin_ref[...], sin_ref[...]] * heads, axis=1)
    rotated = (turned * cos + swapped * sin).astype(BF16)
    blank = jnp.zeros((rows, out_ref.shape[1] - width - rope_dim), BF16)
    copy.wait()
    total = None
    for j in range(heads):
        part = dot(query[:, j * nope_dim : (j + 1) * nope_dim], uk_ref[j]).astype(BF16)
        part = jnp.concatenate([part, rotated[:, j * rope_dim : (j + 1) * rope_dim], blank], axis=1)
        place = one_hot(
            rows * heads, rows, lambda i: i // heads, lambda i, j=j: i % heads == j
        )
        term = dot(place, part)
        total = term if total is None else total + term
    out_ref[...] = total.astype(BF16)


def project(latent, pieces, w_uk, cos, sin):
    heads, _, width = w_uk.shape
    rows = latent.shape[1]
    count = len(pieces)
    full = width + 128 * pl.cdiv(2 * cos.shape[1], 128)

    def kernel(*refs):
        project_kernel(count, *refs)

    return pl.pallas_call(
        kernel,
        out_shape=jax.ShapeDtypeStruct((rows * heads, full), BF16),
        in_specs=[WHOLE] * (1 + count) + [IN_HBM] + [WHOLE] * 2,
        out_specs=WHOLE,
        scratch_shapes=[pltpu.VMEM(w_uk.shape, BF16), pltpu.SemaphoreType.DMA(())],
        compiler_params=params(16),
        name="project",
    )(latent, *pieces, in_hbm(w_uk), cos, sin)


def attend_kernel(
    heads,     length_ref, table_ref, query_ref, new_ref, new_rope_ref, latent_hbm, rope_ref, out_ref,
    scores_ref, held_ref, high_ref, absorbed_ref, rotary_ref, row_ref, slot_ref, sem,
):
    own, slots = table_ref.shape
    pool, page, width = held_ref.shape
    rope_dim = rope_ref.shape[1]
    rows = query_ref.shape[0]
    all_heads = rows // own
    factor = math.log2(math.e) / (NOPE + rope_dim) ** 0.5
    share = pool // CHUNKS
    copies = []
    for c in range(CHUNKS):
        span = pl.ds(c * share, share)
        copies.append(pltpu.make_async_copy(latent_hbm.at[span], held_ref.at[span], sem.at[c]))
    for copy in copies:
        copy.start()
    for r in range(own):
        for i in range(slots):
            index = table_ref[r, i]
            row_ref[index] = r
            slot_ref[index] = i
    def sorted_place(i):
        return (i % all_heads) // heads * (own * heads) + i // all_heads * heads + i % heads

    ordered = dot(one_hot(rows, rows, sorted_place), query_ref[...]).astype(BF16)
    new_scores = []
    for r in range(own):
        q_abs = ordered[r * all_heads : (r + 1) * all_heads, :width]
        q_rot = ordered[r * all_heads : (r + 1) * all_heads, width : width + rope_dim]
        absorbed_ref[r] = q_abs
        rotary_ref[r] = q_rot
        new_rope = new_rope_ref[r : r + 1, :].astype(F32)
        score_new = jnp.sum(
            q_abs.astype(F32) * new_ref[r : r + 1, :].astype(F32), axis=1, keepdims=True
        )
        score_new += jnp.sum(q_rot.astype(F32) * new_rope, axis=1, keepdims=True)
        new_scores.append(score_new * factor)
    high_ref[...] = jnp.full(high_ref.shape, -jnp.inf, F32)
    for c in range(CHUNKS):
        copies[c].wait()
        for g in range(c * share, (c + 1) * share):
            r, i = row_ref[g], slot_ref[g]
            scores = lax.dot_general(
                absorbed_ref[r], held_ref[g], (((1,), (1,)), ((), ())), preferred_element_type=F32
            )
            scores = (scores + dot(rotary_ref[r], rope_ref[g])) * factor
            position = i * page + lax.broadcasted_iota(jnp.int32, scores.shape, 1)
            scores = jnp.where(position < length_ref[r], scores, -jnp.inf)
            scores_ref[r, i] = scores
            high_ref[r] = jnp.maximum(high_ref[r], scores)
    done = []
    for r in range(own):
        score_new = new_scores[r]
        top = jnp.maximum(score_new, jnp.max(high_ref[r], axis=1, keepdims=True))
        weight_new = jnp.exp2(score_new - top)
        total = None
        for i in range(slots):
            weights = jnp.exp2(scores_ref[r, i] - top)
            scores_ref[r, i] = weights
            total = weights if total is None else total + weights
        inverse = 1.0 / (jnp.sum(total, axis=1, keepdims=True) + weight_new)
        new = new_ref[r : r + 1, :].astype(F32)
        summed = (weight_new * inverse).astype(BF16).astype(F32) * new
        for i in range(0, slots, GROUP):
            group = range(i, i + GROUP)
            probs = jnp.concatenate(
                [(scores_ref[r, k] * inverse).astype(BF16) for k in group], axis=1
            )
            latents = jnp.concatenate([held_ref[table_ref[r, k]] for k in group], axis=0)
            summed += dot(probs, latents)
        done.append(summed.astype(BF16))
    def place(i):
        row = i % (own * heads) // heads
        return row * all_heads + i // (own * heads) * heads + i % heads

    out_ref[...] = dot(one_hot(rows, rows, place), jnp.concatenate(done, axis=0)).astype(BF16)


def attend(lengths, table, query, heads, new_latent, new_rope, cache_latent, cache_rope):
    own, slots = table.shape
    pool, page, width = cache_latent.shape
    rope_dim = cache_rope.shape[1]
    rows = query.shape[0]
    all_heads = rows // own

    def kernel(*refs):
        attend_kernel(heads, *refs)

    return pl.pallas_call(
        kernel,
        out_shape=jax.ShapeDtypeStruct((rows, width), BF16),
        in_specs=[SCALARS, SCALARS] + [WHOLE] * 3 + [IN_HBM, WHOLE],
        out_specs=WHOLE,
        scratch_shapes=[
            pltpu.VMEM((own, slots, all_heads, page), F32),
            pltpu.VMEM(cache_latent.shape, BF16),
            pltpu.VMEM((own, all_heads, page), F32),
            pltpu.VMEM((own, all_heads, width), BF16),
            pltpu.VMEM((own, all_heads, rope_dim), BF16),
            pltpu.SMEM((pool,), jnp.int32),
            pltpu.SMEM((pool,), jnp.int32),
            pltpu.SemaphoreType.DMA((CHUNKS,)),
        ],
        compiler_params=params(24),
        name="attend",
    )(lengths, table, query, new_latent, new_rope, in_hbm(cache_latent), cache_rope)


def values_kernel(parts, attn_ref, uv_hbm, out_ref, uv_ref, sem):
    copy = pltpu.make_async_copy(uv_hbm, uv_ref, sem)
    copy.start()
    heads, width, value_dim = uv_ref.shape
    per = value_dim // parts
    count = attn_ref.shape[0]
    rows = count // heads
    place = one_hot(count, count, lambda i: i % rows * heads + i // rows)
    ordered = dot(place, attn_ref[...]).astype(BF16)
    columns = heads * value_dim
    source = lax.broadcasted_iota(jnp.int32, (columns, columns), 0)
    column = lax.broadcasted_iota(jnp.int32, (columns, columns), 1)
    inner = source % value_dim
    target = (inner // per) * (heads * per) + (source // value_dim) * per + inner % per
    move = (column == target).astype(F32).astype(BF16)
    copy.wait()
    value = jnp.concatenate(
        [dot(ordered[j * rows : (j + 1) * rows], uv_ref[j]).astype(BF16) for j in range(heads)],
        axis=1,
    )
    out_ref[...] = dot(value, move).astype(BF16)


def project_values(attn, w_uv, parts):
    heads, _, value_dim = w_uv.shape

    def kernel(*refs):
        values_kernel(parts, *refs)

    return pl.pallas_call(
        kernel,
        out_shape=jax.ShapeDtypeStruct((attn.shape[0] // heads, heads * value_dim), BF16),
        in_specs=[WHOLE, IN_HBM],
        out_specs=WHOLE,
        scratch_shapes=[pltpu.VMEM(w_uv.shape, BF16), pltpu.SemaphoreType.DMA(())],
        compiler_params=params(16),
        name="values",
    )(attn, in_hbm(w_uv))


def mix_kernel(values_ref, weights_ref, out_ref, held_ref, sem):
    steps, sources, per, columns = weights_ref.shape
    depth = sources * per
    copies = [
        pltpu.make_async_copy(weights_ref.at[d], held_ref.at[d], sem.at[d]) for d in range(steps)
    ]
    for copy in copies:
        copy.start()
    total = None
    for d in range(steps):
        copies[d].wait()
        block = held_ref[d].reshape(depth, columns)
        part = jnp.concatenate(
            [values_ref[y, :, d * per : (d + 1) * per] for y in range(sources)], axis=1
        )
        term = dot(part, block)
        total = term if total is None else total + term
    parts, _, width = out_ref.shape
    for z in range(parts):
        out_ref[z] = total[:, z * width : (z + 1) * width].astype(BF16)


def mix(values, weights, parts):
    rows = values.shape[1]
    steps, _, _, columns = weights.shape
    return pl.pallas_call(
        mix_kernel,
        out_shape=jax.ShapeDtypeStruct((parts, rows, columns // parts), BF16),
        in_specs=[WHOLE, IN_HBM],
        out_specs=WHOLE,
        scratch_shapes=[
            pltpu.VMEM(weights.shape, BF16),
            pltpu.SemaphoreType.DMA((steps,)),
        ],
        compiler_params=params(20),
        name="mix",
    )(values, in_hbm(weights))


def finish_kernel(terms_ref, out_ref):
    total = terms_ref[0].astype(F32)
    for z in range(1, terms_ref.shape[0]):
        total += terms_ref[z].astype(F32)
    out_ref[...] = total.astype(BF16)


def finish(terms):
    return pl.pallas_call(
        finish_kernel,
        out_shape=jax.ShapeDtypeStruct(terms.shape[1:], BF16),
        in_specs=[WHOLE],
        out_specs=WHOLE,
        compiler_params=params(8),
        name="finish",
    )(terms)


def shift_dp(x, along, across):
    chips = lax.axis_size("dp") // 2
    pairs = [
        (p * 2 + c, (p + along * (1 - 2 * c)) % chips * 2 + (c ^ across))
        for p in range(chips)
        for c in range(2)
    ]
    return lax.ppermute(x, "dp", pairs)


def shift_y(x, along):
    pairs = [(y * Z + z, (y + along) % Y * Z + z) for y in range(Y) for z in range(Z)]
    return lax.ppermute(x, "head", pairs)


def piece_places():
    me = lax.axis_index("dp")
    chips = lax.axis_size("dp") // 2
    chip, core = me // 2, me % 2
    sign = 1 - 2 * core
    other = lax.rem(core + 1, 2)
    origins = [lax.rem(chip + sign * step + chips, chips) * 2 + core for step in (0, -1, 1, 2)]
    origins += [lax.rem(chip - sign * step + 2 * chips, chips) * 2 + other for step in (0, -1, 1, 2)]
    origins = jnp.stack(origins)
    parts = jnp.arange(2 * chips)
    return jnp.sum(
        jnp.where(origins[None, :] == parts[:, None], parts[None, :], 0), axis=1
    ).astype(jnp.int32)


def angles(lengths, rope_dim):
    half = rope_dim // 2
    freq = 10000.0 ** (-2.0 * jnp.arange(half, dtype=F32) / (2 * half))
    angle = lengths.astype(F32)[:, None] * freq
    return jnp.cos(angle), jnp.sin(angle)


def body(
    q_latent,
    w_qnope,
    w_qrope,
    w_uk,
    w_uv,
    w_out,
    cache_latent,
    cache_rope,
    new_latent,
    new_rope,
    lengths,
    page_table,
):
    rows = q_latent.shape[0]
    heads = w_uk.shape[0]
    own = page_table.shape[0]
    width_all = w_out.shape[2]
    dp_count = lax.axis_size("dp")
    sources = lax.axis_size("head")
    depth = w_out.shape[0] * w_out.shape[1]

    head = lax.axis_index("head")
    y = head // Z
    cos, sin = angles(lengths, cache_rope.shape[1])
    y_scalar = y.reshape(1)
    flat = w_out.reshape(depth, width_all)
    both, *cuts = prepare(y_scalar, w_qnope, w_qrope, flat)
    ahead, behind, beside = shift_dp(both, 1, 0), shift_dp(both, -1, 0), shift_dp(both, 0, 1)
    cuts[2], cuts[1] = shift_y(cuts[2], 2), shift_y(cuts[1], 1)
    latent = arrange(piece_places(), q_latent)
    ahead, behind, beside, cuts, cos, sin, latent = lax.optimization_barrier(
        (ahead, behind, beside, cuts, cos, sin, latent)
    )
    far = shift_dp(ahead, 1, 0)
    ahead_beside, behind_beside = shift_dp(ahead, 0, 1), shift_dp(behind, 0, 1)
    cuts[3] = shift_y(cuts[3], 3)
    far, cuts, ahead_beside, behind_beside = lax.optimization_barrier(
        (far, cuts, ahead_beside, behind_beside)
    )
    pieces = [both, ahead, behind, far, beside]
    pieces += [ahead_beside, behind_beside, shift_dp(far, 0, 1)]
    cuts, pieces = lax.optimization_barrier((cuts, pieces))
    panel = lax.all_gather(stack(y_scalar, cuts), "dp", axis=0)
    query = project(latent, pieces, w_uk, cos, sin)
    query = query.reshape(sources, own * heads, query.shape[1])
    query = lax.all_to_all(query, "head", 0, 0, tiled=True).reshape(rows * heads, -1)
    own_lengths = lax.dynamic_slice_in_dim(lengths, head * own, own)
    attn = attend(
        own_lengths, page_table, query, heads, new_latent, new_rope, cache_latent, cache_rope
    )
    attn = attn.reshape(sources, own * heads, attn.shape[1])
    attn = lax.all_to_all(attn, "head", 0, 0, tiled=True).reshape(rows * heads, -1)
    values = project_values(attn, w_uv, dp_count)
    values = jnp.broadcast_to(values[None], (Y,) + values.shape)
    values = lax.all_to_all(values, "head", 0, 0, tiled=True, axis_index_groups=Y_GROUPS)
    term = mix(values, panel, Z)
    term = lax.all_to_all(term, "head", 0, 0, tiled=True, axis_index_groups=Z_GROUPS)
    return finish(term)


def solution(mesh):
    in_specs = (
        P("dp", None),
        P("dp", "head"),
        P("dp", "head"),
        P("head", None, None),
        P("head", None, None),
        P("head", "dp", None),
        P(("dp", "head"), None, None),
        P(("dp", "head"), None, None),
        P(("dp", "head"), None),
        P(("dp", "head"), None),
        P("dp"),
        P(("dp", "head"), None),
    )
    out_specs = P("dp", "head")
    return jax.shard_map(body, mesh=mesh, in_specs=in_specs, out_specs=out_specs, check_vma=False)
```

```python
import math

import jax
import jax.numpy as jnp
from jax import lax
from jax.experimental import pallas as pl
from jax.experimental.pallas import tpu as pltpu
from jax.sharding import PartitionSpec as P

GROUP = 4
CHUNKS = 4
NOPE = 128
Y = 4
Z = 8
Z_GROUPS = [[y * Z + z for z in range(Z)] for y in range(Y)]
Y_GROUPS = [[y * Z + z for y in range(Y)] for z in range(Z)]
F32 = jnp.float32
BF16 = jnp.bfloat16
WHOLE = pl.BlockSpec(memory_space=pltpu.VMEM)
SCALARS = pl.BlockSpec(memory_space=pltpu.SMEM)
IN_HBM = pl.BlockSpec(memory_space=pltpu.HBM)


def dot(a, b):
    return jnp.dot(a, b, preferred_element_type=F32)


def in_hbm(x):
    return pltpu.with_memory_space_constraint(x, pltpu.HBM)


def params(mib):
    return pltpu.CompilerParams(vmem_limit_bytes=mib * 1024 * 1024)


def prepare_kernel(y_ref, nope_hbm, rope_hbm, weights_hbm, both_ref, *refs):
    cut_refs, sem = refs[: Y - 1], refs[Y - 1]
    width = nope_hbm.shape[1]
    columns = cut_refs[0].shape[1]
    copies = [
        pltpu.make_async_copy(nope_hbm, both_ref.at[:, :width], sem.at[0]),
        pltpu.make_async_copy(rope_hbm, both_ref.at[:, width:], sem.at[1]),
    ]
    for k in range(1, Y):
        start = pl.multiple_of(lax.rem(y_ref[0] + k, Y) * columns, 128)
        source = weights_hbm.at[:, pl.ds(start, columns)]
        copies.append(pltpu.make_async_copy(source, cut_refs[k - 1], sem.at[1 + k]))
    for copy in copies:
        copy.start()
    for copy in copies:
        copy.wait()


def prepare(y, w_qnope, w_qrope, weights):
    depth = w_qnope.shape[0]
    cut = jax.ShapeDtypeStruct((weights.shape[0], weights.shape[1] // Y), BF16)
    return pl.pallas_call(
        prepare_kernel,
        out_shape=(jax.ShapeDtypeStruct((depth, w_qnope.shape[1] + w_qrope.shape[1]), BF16),)
        + (cut,) * (Y - 1),
        in_specs=[SCALARS] + [IN_HBM] * 3,
        out_specs=(WHOLE,) * Y,
        scratch_shapes=[pltpu.SemaphoreType.DMA((1 + Y,))],
        compiler_params=params(8),
        name="prepare",
    )(y, *[in_hbm(a) for a in (w_qnope, w_qrope, weights)])


def arrange_kernel(place_ref, latent_hbm, uk_hbm, out_ref, uk_ref, held_ref, sem):
    copies = [
        pltpu.make_async_copy(latent_hbm, held_ref, sem.at[0]),
        pltpu.make_async_copy(uk_hbm, uk_ref, sem.at[1]),
    ]
    for copy in copies:
        copy.start()
    copies[0].wait()
    parts, _, depth = out_ref.shape
    for d in range(parts):
        out_ref[place_ref[d]] = held_ref[:, d * depth : (d + 1) * depth]
    copies[1].wait()


def arrange(place, latent, w_uk):
    rows, width = latent.shape
    parts = place.shape[0]
    return pl.pallas_call(
        arrange_kernel,
        out_shape=(
            jax.ShapeDtypeStruct((parts, rows, width // parts), BF16),
            jax.ShapeDtypeStruct(w_uk.shape, BF16),
        ),
        in_specs=[SCALARS] + [IN_HBM] * 2,
        out_specs=(WHOLE, WHOLE),
        scratch_shapes=[pltpu.VMEM(latent.shape, BF16), pltpu.SemaphoreType.DMA((2,))],
        compiler_params=params(8),
        name="arrange",
    )(place, in_hbm(latent), in_hbm(w_uk))


def stack_kernel(y_ref, weights_hbm, *refs):
    pieces, (out_ref, own_ref, sem) = refs[: Y - 1], refs[Y - 1 :]
    y = y_ref[0]
    columns = own_ref.shape[1]
    span = pl.ds(pl.multiple_of(y * columns, 128), columns)
    own = pltpu.make_async_copy(weights_hbm.at[:, span], own_ref, sem.at[0])
    own.start()
    copies = []
    for k in range(1, Y):
        target = out_ref.at[lax.rem(y + (Y - k), Y)]
        copies.append(pltpu.make_async_copy(pieces[k - 1], target, sem.at[k]))
        copies[-1].start()
    own.wait()
    copies.append(pltpu.make_async_copy(own_ref, out_ref.at[y], sem.at[Y]))
    copies[-1].start()
    for copy in copies:
        copy.wait()


def stack(y, weights, pieces):
    return pl.pallas_call(
        stack_kernel,
        out_shape=jax.ShapeDtypeStruct((Y,) + pieces[0].shape, BF16),
        in_specs=[SCALARS, IN_HBM] + [pl.BlockSpec(memory_space=pl.ANY)] * (Y - 1),
        out_specs=IN_HBM,
        scratch_shapes=[pltpu.VMEM(pieces[0].shape, BF16), pltpu.SemaphoreType.DMA((Y + 1,))],
        compiler_params=params(8),
        name="stack",
    )(y, in_hbm(weights), *pieces)


def one_hot(rows, columns, place, keep=None):
    a = lax.broadcasted_iota(jnp.int32, (rows, columns), 0)
    b = lax.broadcasted_iota(jnp.int32, (rows, columns), 1)
    hit = place(a) == b
    if keep is not None:
        hit = hit & keep(a)
    return hit.astype(F32).astype(BF16)


def project_kernel(pieces, latent_ref, *refs):
    piece_refs = refs[:pieces]
    uk_ref, cos_ref, sin_ref, out_ref = refs[pieces:]
    heads, nope_dim, width = uk_ref.shape
    rows = latent_ref.shape[1]
    both = None
    for i in range(pieces):
        term = dot(latent_ref[i], piece_refs[i][...])
        both = term if both is None else both + term
    query = both[:, : heads * nope_dim].astype(BF16)
    turned = both[:, heads * nope_dim :]
    lanes = turned.shape[1]
    rope_dim = lanes // heads
    lane = lax.broadcasted_iota(jnp.int32, turned.shape, 1)
    half = rope_dim // 2
    swapped = jnp.where(
        lane % rope_dim < half,
        pltpu.roll(turned, lanes - half, 1),
        pltpu.roll(turned, half, 1),
    )
    cos = jnp.concatenate([cos_ref[...]] * (2 * heads), axis=1)
    sin = jnp.concatenate([-sin_ref[...], sin_ref[...]] * heads, axis=1)
    rotated = (turned * cos + swapped * sin).astype(BF16)
    blank = jnp.zeros((rows, out_ref.shape[1] - width - rope_dim), BF16)
    total = None
    for j in range(heads):
        part = dot(query[:, j * nope_dim : (j + 1) * nope_dim], uk_ref[j]).astype(BF16)
        part = jnp.concatenate([part, rotated[:, j * rope_dim : (j + 1) * rope_dim], blank], axis=1)
        place = one_hot(
            rows * heads, rows, lambda i: i // heads, lambda i, j=j: i % heads == j
        )
        term = dot(place, part)
        total = term if total is None else total + term
    out_ref[...] = total.astype(BF16)


def project(latent, pieces, w_uk, cos, sin):
    heads, _, width = w_uk.shape
    rows = latent.shape[1]
    count = len(pieces)
    full = width + 128 * pl.cdiv(2 * cos.shape[1], 128)

    def kernel(*refs):
        project_kernel(count, *refs)

    return pl.pallas_call(
        kernel,
        out_shape=jax.ShapeDtypeStruct((rows * heads, full), BF16),
        in_specs=[WHOLE] * (4 + count),
        out_specs=WHOLE,
        compiler_params=params(16),
        name="project",
    )(latent, *pieces, w_uk, cos, sin)


def attend_kernel(
    heads,     length_ref, table_ref, query_ref, new_ref, new_rope_ref, latent_hbm, rope_hbm, out_ref,
    scores_ref, held_ref, rope_ref, high_ref, absorbed_ref, rotary_ref, row_ref, slot_ref, sem,
):
    own, slots = table_ref.shape
    pool, page, width = held_ref.shape
    rope_dim = rope_ref.shape[1]
    rows = query_ref.shape[0]
    all_heads = rows // own
    factor = math.log2(math.e) / (NOPE + rope_dim) ** 0.5
    share = pool // CHUNKS
    copies = []
    for c in range(CHUNKS):
        span = pl.ds(c * share, share)
        copies.append(pltpu.make_async_copy(latent_hbm.at[span], held_ref.at[span], sem.at[c]))
    rope_copy = pltpu.make_async_copy(rope_hbm, rope_ref, sem.at[CHUNKS])
    rope_copy.start()
    for copy in copies:
        copy.start()
    for r in range(own):
        for i in range(slots):
            index = table_ref[r, i]
            row_ref[index] = r
            slot_ref[index] = i
    def sorted_place(i):
        return (i % all_heads) // heads * (own * heads) + i // all_heads * heads + i % heads

    ordered = dot(one_hot(rows, rows, sorted_place), query_ref[...]).astype(BF16)
    new_scores = []
    for r in range(own):
        q_abs = ordered[r * all_heads : (r + 1) * all_heads, :width]
        q_rot = ordered[r * all_heads : (r + 1) * all_heads, width : width + rope_dim]
        absorbed_ref[r] = q_abs
        rotary_ref[r] = q_rot
        new_rope = new_rope_ref[r : r + 1, :].astype(F32)
        score_new = jnp.sum(
            q_abs.astype(F32) * new_ref[r : r + 1, :].astype(F32), axis=1, keepdims=True
        )
        score_new += jnp.sum(q_rot.astype(F32) * new_rope, axis=1, keepdims=True)
        new_scores.append(score_new * factor)
    high_ref[...] = jnp.full(high_ref.shape, -jnp.inf, F32)
    rope_copy.wait()
    for c in range(CHUNKS):
        copies[c].wait()
        for g in range(c * share, (c + 1) * share):
            r, i = row_ref[g], slot_ref[g]
            scores = lax.dot_general(
                absorbed_ref[r], held_ref[g], (((1,), (1,)), ((), ())), preferred_element_type=F32
            )
            scores = (scores + dot(rotary_ref[r], rope_ref[g])) * factor
            position = i * page + lax.broadcasted_iota(jnp.int32, scores.shape, 1)
            scores = jnp.where(position < length_ref[r], scores, -jnp.inf)
            scores_ref[r, i] = scores
            high_ref[r] = jnp.maximum(high_ref[r], scores)
    done = []
    for r in range(own):
        score_new = new_scores[r]
        top = jnp.maximum(score_new, jnp.max(high_ref[r], axis=1, keepdims=True))
        weight_new = jnp.exp2(score_new - top)
        total = None
        for i in range(slots):
            weights = jnp.exp2(scores_ref[r, i] - top)
            scores_ref[r, i] = weights
            total = weights if total is None else total + weights
        inverse = 1.0 / (jnp.sum(total, axis=1, keepdims=True) + weight_new)
        new = new_ref[r : r + 1, :].astype(F32)
        summed = (weight_new * inverse).astype(BF16).astype(F32) * new
        for i in range(0, slots, GROUP):
            group = range(i, i + GROUP)
            probs = jnp.concatenate(
                [(scores_ref[r, k] * inverse).astype(BF16) for k in group], axis=1
            )
            latents = jnp.concatenate([held_ref[table_ref[r, k]] for k in group], axis=0)
            summed += dot(probs, latents)
        done.append(summed.astype(BF16))
    def place(i):
        row = i % (own * heads) // heads
        return row * all_heads + i // (own * heads) * heads + i % heads

    out_ref[...] = dot(one_hot(rows, rows, place), jnp.concatenate(done, axis=0)).astype(BF16)


def attend(lengths, table, query, heads, new_latent, new_rope, cache_latent, cache_rope):
    own, slots = table.shape
    pool, page, width = cache_latent.shape
    rope_dim = cache_rope.shape[1]
    rows = query.shape[0]
    all_heads = rows // own

    def kernel(*refs):
        attend_kernel(heads, *refs)

    return pl.pallas_call(
        kernel,
        out_shape=jax.ShapeDtypeStruct((rows, width), BF16),
        in_specs=[SCALARS, SCALARS] + [WHOLE] * 3 + [IN_HBM, IN_HBM],
        out_specs=WHOLE,
        scratch_shapes=[
            pltpu.VMEM((own, slots, all_heads, page), F32),
            pltpu.VMEM(cache_latent.shape, BF16),
            pltpu.VMEM(cache_rope.shape, BF16),
            pltpu.VMEM((own, all_heads, page), F32),
            pltpu.VMEM((own, all_heads, width), BF16),
            pltpu.VMEM((own, all_heads, rope_dim), BF16),
            pltpu.SMEM((pool,), jnp.int32),
            pltpu.SMEM((pool,), jnp.int32),
            pltpu.SemaphoreType.DMA((CHUNKS + 1,)),
        ],
        compiler_params=params(24),
        name="attend",
    )(lengths, table, query, new_latent, new_rope, in_hbm(cache_latent), in_hbm(cache_rope))


def values_kernel(parts, attn_ref, uv_hbm, out_ref, uv_ref, sem):
    copy = pltpu.make_async_copy(uv_hbm, uv_ref, sem)
    copy.start()
    heads, width, value_dim = uv_ref.shape
    per = value_dim // parts
    count = attn_ref.shape[0]
    rows = count // heads
    place = one_hot(count, count, lambda i: i % rows * heads + i // rows)
    ordered = dot(place, attn_ref[...]).astype(BF16)
    columns = heads * value_dim
    source = lax.broadcasted_iota(jnp.int32, (columns, columns), 0)
    column = lax.broadcasted_iota(jnp.int32, (columns, columns), 1)
    inner = source % value_dim
    target = (inner // per) * (heads * per) + (source // value_dim) * per + inner % per
    move = (column == target).astype(F32).astype(BF16)
    copy.wait()
    value = jnp.concatenate(
        [dot(ordered[j * rows : (j + 1) * rows], uv_ref[j]).astype(BF16) for j in range(heads)],
        axis=1,
    )
    out_ref[...] = dot(value, move).astype(BF16)


def project_values(attn, w_uv, parts):
    heads, _, value_dim = w_uv.shape

    def kernel(*refs):
        values_kernel(parts, *refs)

    return pl.pallas_call(
        kernel,
        out_shape=jax.ShapeDtypeStruct((attn.shape[0] // heads, heads * value_dim), BF16),
        in_specs=[WHOLE, IN_HBM],
        out_specs=WHOLE,
        scratch_shapes=[pltpu.VMEM(w_uv.shape, BF16), pltpu.SemaphoreType.DMA(())],
        compiler_params=params(16),
        name="values",
    )(attn, in_hbm(w_uv))


def mix_kernel(values_ref, weights_ref, out_ref, held_ref, sem):
    steps, sources, per, columns = weights_ref.shape
    depth = sources * per
    copies = [
        pltpu.make_async_copy(weights_ref.at[d], held_ref.at[d], sem.at[d]) for d in range(steps)
    ]
    for copy in copies:
        copy.start()
    total = None
    for d in range(steps):
        copies[d].wait()
        block = held_ref[d].reshape(depth, columns)
        part = jnp.concatenate(
            [values_ref[y, :, d * per : (d + 1) * per] for y in range(sources)], axis=1
        )
        term = dot(part, block)
        total = term if total is None else total + term
    parts, _, width = out_ref.shape
    for z in range(parts):
        out_ref[z] = total[:, z * width : (z + 1) * width].astype(BF16)


def mix(values, weights, parts):
    rows = values.shape[1]
    steps, _, _, columns = weights.shape
    return pl.pallas_call(
        mix_kernel,
        out_shape=jax.ShapeDtypeStruct((parts, rows, columns // parts), BF16),
        in_specs=[WHOLE, IN_HBM],
        out_specs=WHOLE,
        scratch_shapes=[
            pltpu.VMEM(weights.shape, BF16),
            pltpu.SemaphoreType.DMA((steps,)),
        ],
        compiler_params=params(20),
        name="mix",
    )(values, in_hbm(weights))


def finish_kernel(terms_ref, out_ref):
    total = terms_ref[0].astype(F32)
    for z in range(1, terms_ref.shape[0]):
        total += terms_ref[z].astype(F32)
    out_ref[...] = total.astype(BF16)


def finish(terms):
    return pl.pallas_call(
        finish_kernel,
        out_shape=jax.ShapeDtypeStruct(terms.shape[1:], BF16),
        in_specs=[WHOLE],
        out_specs=WHOLE,
        compiler_params=params(8),
        name="finish",
    )(terms)


def shift_dp(x, along, across):
    chips = lax.axis_size("dp") // 2
    pairs = [
        (p * 2 + c, (p + along * (1 - 2 * c)) % chips * 2 + (c ^ across))
        for p in range(chips)
        for c in range(2)
    ]
    return lax.ppermute(x, "dp", pairs)


def shift_y(x, along):
    pairs = [(y * Z + z, (y + along) % Y * Z + z) for y in range(Y) for z in range(Z)]
    return lax.ppermute(x, "head", pairs)


def piece_places():
    me = lax.axis_index("dp")
    chips = lax.axis_size("dp") // 2
    chip, core = me // 2, me % 2
    sign = 1 - 2 * core
    other = lax.rem(core + 1, 2)
    origins = [lax.rem(chip + sign * step + chips, chips) * 2 + core for step in (0, -1, 1, 2)]
    origins += [lax.rem(chip - sign * step + 2 * chips, chips) * 2 + other for step in (0, -1, 1, 2)]
    origins = jnp.stack(origins)
    parts = jnp.arange(2 * chips)
    return jnp.sum(
        jnp.where(origins[None, :] == parts[:, None], parts[None, :], 0), axis=1
    ).astype(jnp.int32)


def angles(lengths, rope_dim):
    half = rope_dim // 2
    freq = 10000.0 ** (-2.0 * jnp.arange(half, dtype=F32) / (2 * half))
    angle = lengths.astype(F32)[:, None] * freq
    return jnp.cos(angle), jnp.sin(angle)


def body(
    q_latent,
    w_qnope,
    w_qrope,
    w_uk,
    w_uv,
    w_out,
    cache_latent,
    cache_rope,
    new_latent,
    new_rope,
    lengths,
    page_table,
):
    rows = q_latent.shape[0]
    heads = w_uk.shape[0]
    own = page_table.shape[0]
    width_all = w_out.shape[2]
    dp_count = lax.axis_size("dp")
    sources = lax.axis_size("head")
    depth = w_out.shape[0] * w_out.shape[1]

    head = lax.axis_index("head")
    y = head // Z
    cos, sin = angles(lengths, cache_rope.shape[1])
    y_scalar = y.reshape(1)
    flat = w_out.reshape(depth, width_all)
    both, *cuts = prepare(y_scalar, w_qnope, w_qrope, flat)
    ahead, behind, beside = shift_dp(both, 1, 0), shift_dp(both, -1, 0), shift_dp(both, 0, 1)
    cuts[1] = shift_y(cuts[1], 2)
    latent, uk = arrange(piece_places(), q_latent, w_uk)
    ahead, behind, beside, cuts, cos, sin, latent, uk = lax.optimization_barrier(
        (ahead, behind, beside, cuts, cos, sin, latent, uk)
    )
    far = shift_dp(ahead, 1, 0)
    ahead_beside, behind_beside = shift_dp(ahead, 0, 1), shift_dp(behind, 0, 1)
    cuts[0], cuts[2] = shift_y(cuts[0], 1), shift_y(cuts[2], 3)
    far, cuts, ahead_beside, behind_beside = lax.optimization_barrier(
        (far, cuts, ahead_beside, behind_beside)
    )
    pieces = [both, ahead, behind, far, beside]
    pieces += [ahead_beside, behind_beside, shift_dp(far, 0, 1)]
    cuts, pieces = lax.optimization_barrier((cuts, pieces))
    panel = lax.all_gather(stack(y_scalar, flat, cuts), "dp", axis=0)
    query = project(latent, pieces, uk, cos, sin)
    query = query.reshape(sources, own * heads, query.shape[1])
    query = lax.all_to_all(query, "head", 0, 0, tiled=True).reshape(rows * heads, -1)
    own_lengths = lax.dynamic_slice_in_dim(lengths, head * own, own)
    attn = attend(
        own_lengths, page_table, query, heads, new_latent, new_rope, cache_latent, cache_rope
    )
    attn = attn.reshape(sources, own * heads, attn.shape[1])
    attn = lax.all_to_all(attn, "head", 0, 0, tiled=True).reshape(rows * heads, -1)
    values = project_values(attn, w_uv, dp_count)
    values = jnp.broadcast_to(values[None], (Y,) + values.shape)
    values = lax.all_to_all(values, "head", 0, 0, tiled=True, axis_index_groups=Y_GROUPS)
    term = mix(values, panel, Z)
    term = lax.all_to_all(term, "head", 0, 0, tiled=True, axis_index_groups=Z_GROUPS)
    return finish(term)


def solution(mesh):
    in_specs = (
        P("dp", None),
        P("dp", "head"),
        P("dp", "head"),
        P("head", None, None),
        P("head", None, None),
        P("head", "dp", None),
        P(("dp", "head"), None, None),
        P(("dp", "head"), None, None),
        P(("dp", "head"), None),
        P(("dp", "head"), None),
        P("dp"),
        P(("dp", "head"), None),
    )
    out_specs = P("dp", "head")
    return jax.shard_map(body, mesh=mesh, in_specs=in_specs, out_specs=out_specs, check_vma=False)
```

```python
import math

import jax
import jax.numpy as jnp
from jax import lax
from jax.experimental import pallas as pl
from jax.experimental.pallas import tpu as pltpu
from jax.sharding import PartitionSpec as P

GROUP = 4
CHUNKS = 4
NOPE = 128
Y = 4
Z = 8
Z_GROUPS = [[y * Z + z for z in range(Z)] for y in range(Y)]
Y_GROUPS = [[y * Z + z for y in range(Y)] for z in range(Z)]
F32 = jnp.float32
BF16 = jnp.bfloat16
WHOLE = pl.BlockSpec(memory_space=pltpu.VMEM)
SCALARS = pl.BlockSpec(memory_space=pltpu.SMEM)
IN_HBM = pl.BlockSpec(memory_space=pltpu.HBM)


def dot(a, b):
    return jnp.dot(a, b, preferred_element_type=F32)


def in_hbm(x):
    return pltpu.with_memory_space_constraint(x, pltpu.HBM)


def params(mib):
    return pltpu.CompilerParams(vmem_limit_bytes=mib * 1024 * 1024)


def prepare_kernel(y_ref, nope_hbm, rope_hbm, weights_hbm, both_ref, *refs):
    cut_refs, sem = refs[: Y - 1], refs[Y - 1]
    width = nope_hbm.shape[1]
    columns = cut_refs[0].shape[1]
    copies = [
        pltpu.make_async_copy(nope_hbm, both_ref.at[:, :width], sem.at[0]),
        pltpu.make_async_copy(rope_hbm, both_ref.at[:, width:], sem.at[1]),
    ]
    for k in range(1, Y):
        start = pl.multiple_of(lax.rem(y_ref[0] + k, Y) * columns, 128)
        source = weights_hbm.at[:, pl.ds(start, columns)]
        copies.append(pltpu.make_async_copy(source, cut_refs[k - 1], sem.at[1 + k]))
    for copy in copies:
        copy.start()
    for copy in copies:
        copy.wait()


def prepare(y, w_qnope, w_qrope, weights):
    depth = w_qnope.shape[0]
    cut = jax.ShapeDtypeStruct((weights.shape[0], weights.shape[1] // Y), BF16)
    return pl.pallas_call(
        prepare_kernel,
        out_shape=(jax.ShapeDtypeStruct((depth, w_qnope.shape[1] + w_qrope.shape[1]), BF16),)
        + (cut,) * (Y - 1),
        in_specs=[SCALARS] + [IN_HBM] * 3,
        out_specs=(WHOLE,) * Y,
        scratch_shapes=[pltpu.SemaphoreType.DMA((1 + Y,))],
        compiler_params=params(8),
        name="prepare",
    )(y, *[in_hbm(a) for a in (w_qnope, w_qrope, weights)])


def arrange_kernel(place_ref, latent_hbm, uk_hbm, out_ref, uk_ref, held_ref, sem):
    copies = [
        pltpu.make_async_copy(latent_hbm, held_ref, sem.at[0]),
        pltpu.make_async_copy(uk_hbm, uk_ref, sem.at[1]),
    ]
    for copy in copies:
        copy.start()
    copies[0].wait()
    parts, _, depth = out_ref.shape
    for d in range(parts):
        out_ref[place_ref[d]] = held_ref[:, d * depth : (d + 1) * depth]
    copies[1].wait()


def arrange(place, latent, w_uk):
    rows, width = latent.shape
    parts = place.shape[0]
    return pl.pallas_call(
        arrange_kernel,
        out_shape=(
            jax.ShapeDtypeStruct((parts, rows, width // parts), BF16),
            jax.ShapeDtypeStruct(w_uk.shape, BF16),
        ),
        in_specs=[SCALARS] + [IN_HBM] * 2,
        out_specs=(WHOLE, WHOLE),
        scratch_shapes=[pltpu.VMEM(latent.shape, BF16), pltpu.SemaphoreType.DMA((2,))],
        compiler_params=params(8),
        name="arrange",
    )(place, in_hbm(latent), in_hbm(w_uk))


def stack_kernel(y_ref, weights_hbm, *refs):
    pieces, (out_ref, own_ref, sem) = refs[: Y - 1], refs[Y - 1 :]
    y = y_ref[0]
    columns = own_ref.shape[1]
    span = pl.ds(pl.multiple_of(y * columns, 128), columns)
    own = pltpu.make_async_copy(weights_hbm.at[:, span], own_ref, sem.at[0])
    own.start()
    copies = []
    for k in range(1, Y):
        target = out_ref.at[lax.rem(y + (Y - k), Y)]
        copies.append(pltpu.make_async_copy(pieces[k - 1], target, sem.at[k]))
        copies[-1].start()
    own.wait()
    copies.append(pltpu.make_async_copy(own_ref, out_ref.at[y], sem.at[Y]))
    copies[-1].start()
    for copy in copies:
        copy.wait()


def stack(y, weights, pieces):
    return pl.pallas_call(
        stack_kernel,
        out_shape=jax.ShapeDtypeStruct((Y,) + pieces[0].shape, BF16),
        in_specs=[SCALARS, IN_HBM] + [pl.BlockSpec(memory_space=pl.ANY)] * (Y - 1),
        out_specs=IN_HBM,
        scratch_shapes=[pltpu.VMEM(pieces[0].shape, BF16), pltpu.SemaphoreType.DMA((Y + 1,))],
        compiler_params=params(8),
        name="stack",
    )(y, in_hbm(weights), *pieces)


def one_hot(rows, columns, place, keep=None):
    a = lax.broadcasted_iota(jnp.int32, (rows, columns), 0)
    b = lax.broadcasted_iota(jnp.int32, (rows, columns), 1)
    hit = place(a) == b
    if keep is not None:
        hit = hit & keep(a)
    return hit.astype(F32).astype(BF16)


def project_kernel(pieces, latent_ref, *refs):
    piece_refs = refs[:pieces]
    uk_ref, cos_ref, sin_ref, out_ref = refs[pieces:]
    heads, nope_dim, width = uk_ref.shape
    rows = latent_ref.shape[1]
    both = None
    for i in range(pieces):
        term = dot(latent_ref[i], piece_refs[i][...])
        both = term if both is None else both + term
    query = both[:, : heads * nope_dim].astype(BF16)
    turned = both[:, heads * nope_dim :]
    lanes = turned.shape[1]
    rope_dim = lanes // heads
    lane = lax.broadcasted_iota(jnp.int32, turned.shape, 1)
    half = rope_dim // 2
    swapped = jnp.where(
        lane % rope_dim < half,
        pltpu.roll(turned, lanes - half, 1),
        pltpu.roll(turned, half, 1),
    )
    cos = jnp.concatenate([cos_ref[...]] * (2 * heads), axis=1)
    sin = jnp.concatenate([-sin_ref[...], sin_ref[...]] * heads, axis=1)
    rotated = (turned * cos + swapped * sin).astype(BF16)
    blank = jnp.zeros((rows, out_ref.shape[1] - width - rope_dim), BF16)
    total = None
    for j in range(heads):
        part = dot(query[:, j * nope_dim : (j + 1) * nope_dim], uk_ref[j]).astype(BF16)
        part = jnp.concatenate([part, rotated[:, j * rope_dim : (j + 1) * rope_dim], blank], axis=1)
        place = one_hot(
            rows * heads, rows, lambda i: i // heads, lambda i, j=j: i % heads == j
        )
        term = dot(place, part)
        total = term if total is None else total + term
    out_ref[...] = total.astype(BF16)


def project(latent, pieces, w_uk, cos, sin):
    heads, _, width = w_uk.shape
    rows = latent.shape[1]
    count = len(pieces)
    full = width + 128 * pl.cdiv(2 * cos.shape[1], 128)

    def kernel(*refs):
        project_kernel(count, *refs)

    return pl.pallas_call(
        kernel,
        out_shape=jax.ShapeDtypeStruct((rows * heads, full), BF16),
        in_specs=[WHOLE] * (4 + count),
        out_specs=WHOLE,
        compiler_params=params(16),
        name="project",
    )(latent, *pieces, w_uk, cos, sin)


def attend_kernel(
    heads,     length_ref, table_ref, query_ref, new_ref, new_rope_ref, latent_hbm, rope_hbm, out_ref,
    scores_ref, held_ref, rope_ref, high_ref, absorbed_ref, rotary_ref, row_ref, slot_ref, sem,
):
    own, slots = table_ref.shape
    pool, page, width = held_ref.shape
    rope_dim = rope_ref.shape[1]
    rows = query_ref.shape[0]
    all_heads = rows // own
    factor = math.log2(math.e) / (NOPE + rope_dim) ** 0.5
    share = pool // CHUNKS
    copies = []
    for c in range(CHUNKS):
        span = pl.ds(c * share, share)
        copies.append(pltpu.make_async_copy(latent_hbm.at[span], held_ref.at[span], sem.at[c]))
    rope_copy = pltpu.make_async_copy(rope_hbm, rope_ref, sem.at[CHUNKS])
    rope_copy.start()
    for copy in copies:
        copy.start()
    for r in range(own):
        for i in range(slots):
            index = table_ref[r, i]
            row_ref[index] = r
            slot_ref[index] = i
    def sorted_place(i):
        return (i % all_heads) // heads * (own * heads) + i // all_heads * heads + i % heads

    ordered = dot(one_hot(rows, rows, sorted_place), query_ref[...]).astype(BF16)
    new_scores = []
    for r in range(own):
        q_abs = ordered[r * all_heads : (r + 1) * all_heads, :width]
        q_rot = ordered[r * all_heads : (r + 1) * all_heads, width : width + rope_dim]
        absorbed_ref[r] = q_abs
        rotary_ref[r] = q_rot
        new_rope = new_rope_ref[r : r + 1, :].astype(F32)
        score_new = jnp.sum(
            q_abs.astype(F32) * new_ref[r : r + 1, :].astype(F32), axis=1, keepdims=True
        )
        score_new += jnp.sum(q_rot.astype(F32) * new_rope, axis=1, keepdims=True)
        new_scores.append(score_new * factor)
    high_ref[...] = jnp.full(high_ref.shape, -jnp.inf, F32)
    rope_copy.wait()
    for c in range(CHUNKS):
        copies[c].wait()
        for g in range(c * share, (c + 1) * share):
            r, i = row_ref[g], slot_ref[g]
            scores = lax.dot_general(
                absorbed_ref[r], held_ref[g], (((1,), (1,)), ((), ())), preferred_element_type=F32
            )
            scores = (scores + dot(rotary_ref[r], rope_ref[g])) * factor
            position = i * page + lax.broadcasted_iota(jnp.int32, scores.shape, 1)
            scores = jnp.where(position < length_ref[r], scores, -jnp.inf)
            scores_ref[r, i] = scores
            high_ref[r] = jnp.maximum(high_ref[r], scores)
    done = []
    for r in range(own):
        score_new = new_scores[r]
        top = jnp.maximum(score_new, jnp.max(high_ref[r], axis=1, keepdims=True))
        weight_new = jnp.exp2(score_new - top)
        total = None
        for i in range(slots):
            weights = jnp.exp2(scores_ref[r, i] - top)
            scores_ref[r, i] = weights
            total = weights if total is None else total + weights
        inverse = 1.0 / (jnp.sum(total, axis=1, keepdims=True) + weight_new)
        new = new_ref[r : r + 1, :].astype(F32)
        summed = (weight_new * inverse).astype(BF16).astype(F32) * new
        for i in range(0, slots, GROUP):
            group = range(i, i + GROUP)
            probs = jnp.concatenate(
                [(scores_ref[r, k] * inverse).astype(BF16) for k in group], axis=1
            )
            latents = jnp.concatenate([held_ref[table_ref[r, k]] for k in group], axis=0)
            summed += dot(probs, latents)
        done.append(summed.astype(BF16))
    def place(i):
        row = i % (own * heads) // heads
        return row * all_heads + i // (own * heads) * heads + i % heads

    out_ref[...] = dot(one_hot(rows, rows, place), jnp.concatenate(done, axis=0)).astype(BF16)


def attend(lengths, table, query, heads, new_latent, new_rope, cache_latent, cache_rope):
    own, slots = table.shape
    pool, page, width = cache_latent.shape
    rope_dim = cache_rope.shape[1]
    rows = query.shape[0]
    all_heads = rows // own

    def kernel(*refs):
        attend_kernel(heads, *refs)

    return pl.pallas_call(
        kernel,
        out_shape=jax.ShapeDtypeStruct((rows, width), BF16),
        in_specs=[SCALARS, SCALARS] + [WHOLE] * 3 + [IN_HBM, IN_HBM],
        out_specs=WHOLE,
        scratch_shapes=[
            pltpu.VMEM((own, slots, all_heads, page), F32),
            pltpu.VMEM(cache_latent.shape, BF16),
            pltpu.VMEM(cache_rope.shape, BF16),
            pltpu.VMEM((own, all_heads, page), F32),
            pltpu.VMEM((own, all_heads, width), BF16),
            pltpu.VMEM((own, all_heads, rope_dim), BF16),
            pltpu.SMEM((pool,), jnp.int32),
            pltpu.SMEM((pool,), jnp.int32),
            pltpu.SemaphoreType.DMA((CHUNKS + 1,)),
        ],
        compiler_params=params(24),
        name="attend",
    )(lengths, table, query, new_latent, new_rope, in_hbm(cache_latent), in_hbm(cache_rope))


def values_kernel(parts, attn_ref, uv_hbm, out_ref, uv_ref, sem):
    copy = pltpu.make_async_copy(uv_hbm, uv_ref, sem)
    copy.start()
    heads, width, value_dim = uv_ref.shape
    per = value_dim // parts
    count = attn_ref.shape[0]
    rows = count // heads
    place = one_hot(count, count, lambda i: i % rows * heads + i // rows)
    ordered = dot(place, attn_ref[...]).astype(BF16)
    columns = heads * value_dim
    source = lax.broadcasted_iota(jnp.int32, (columns, columns), 0)
    column = lax.broadcasted_iota(jnp.int32, (columns, columns), 1)
    inner = source % value_dim
    target = (inner // per) * (heads * per) + (source // value_dim) * per + inner % per
    move = (column == target).astype(F32).astype(BF16)
    copy.wait()
    value = jnp.concatenate(
        [dot(ordered[j * rows : (j + 1) * rows], uv_ref[j]).astype(BF16) for j in range(heads)],
        axis=1,
    )
    out_ref[...] = dot(value, move).astype(BF16)


def project_values(attn, w_uv, parts):
    heads, _, value_dim = w_uv.shape

    def kernel(*refs):
        values_kernel(parts, *refs)

    return pl.pallas_call(
        kernel,
        out_shape=jax.ShapeDtypeStruct((attn.shape[0] // heads, heads * value_dim), BF16),
        in_specs=[WHOLE, IN_HBM],
        out_specs=WHOLE,
        scratch_shapes=[pltpu.VMEM(w_uv.shape, BF16), pltpu.SemaphoreType.DMA(())],
        compiler_params=params(16),
        name="values",
    )(attn, in_hbm(w_uv))


def mix_kernel(values_ref, weights_ref, out_ref, held_ref, sem):
    steps, sources, per, columns = weights_ref.shape
    depth = sources * per
    spans = [pl.ds(d, 2) for d in range(0, steps, 2)]
    copies = [
        pltpu.make_async_copy(weights_ref.at[span], held_ref.at[span], sem.at[k])
        for k, span in enumerate(spans)
    ]
    for copy in copies:
        copy.start()
    total = None
    for d in range(steps):
        if d % 2 == 0:
            copies[d // 2].wait()
        block = held_ref[d].reshape(depth, columns)
        part = jnp.concatenate(
            [values_ref[y, :, d * per : (d + 1) * per] for y in range(sources)], axis=1
        )
        term = dot(part, block)
        total = term if total is None else total + term
    parts, _, width = out_ref.shape
    for z in range(parts):
        out_ref[z] = total[:, z * width : (z + 1) * width].astype(BF16)


def mix(values, weights, parts):
    rows = values.shape[1]
    steps, _, _, columns = weights.shape
    return pl.pallas_call(
        mix_kernel,
        out_shape=jax.ShapeDtypeStruct((parts, rows, columns // parts), BF16),
        in_specs=[WHOLE, IN_HBM],
        out_specs=WHOLE,
        scratch_shapes=[
            pltpu.VMEM(weights.shape, BF16),
            pltpu.SemaphoreType.DMA((steps // 2,)),
        ],
        compiler_params=params(20),
        name="mix",
    )(values, in_hbm(weights))


def finish_kernel(terms_ref, out_ref):
    total = terms_ref[0].astype(F32)
    for z in range(1, terms_ref.shape[0]):
        total += terms_ref[z].astype(F32)
    out_ref[...] = total.astype(BF16)


def finish(terms):
    return pl.pallas_call(
        finish_kernel,
        out_shape=jax.ShapeDtypeStruct(terms.shape[1:], BF16),
        in_specs=[WHOLE],
        out_specs=WHOLE,
        compiler_params=params(8),
        name="finish",
    )(terms)


def shift_dp(x, along, across):
    chips = lax.axis_size("dp") // 2
    pairs = [
        (p * 2 + c, (p + along * (1 - 2 * c)) % chips * 2 + (c ^ across))
        for p in range(chips)
        for c in range(2)
    ]
    return lax.ppermute(x, "dp", pairs)


def shift_y(x, along):
    pairs = [(y * Z + z, (y + along) % Y * Z + z) for y in range(Y) for z in range(Z)]
    return lax.ppermute(x, "head", pairs)


def piece_places():
    me = lax.axis_index("dp")
    chips = lax.axis_size("dp") // 2
    chip, core = me // 2, me % 2
    sign = 1 - 2 * core
    other = lax.rem(core + 1, 2)
    origins = [lax.rem(chip + sign * step + chips, chips) * 2 + core for step in (0, -1, 1, 2)]
    origins += [lax.rem(chip - sign * step + 2 * chips, chips) * 2 + other for step in (0, -1, 1, 2)]
    origins = jnp.stack(origins)
    parts = jnp.arange(2 * chips)
    return jnp.sum(
        jnp.where(origins[None, :] == parts[:, None], parts[None, :], 0), axis=1
    ).astype(jnp.int32)


def angles(lengths, rope_dim):
    half = rope_dim // 2
    freq = 10000.0 ** (-2.0 * jnp.arange(half, dtype=F32) / (2 * half))
    angle = lengths.astype(F32)[:, None] * freq
    return jnp.cos(angle), jnp.sin(angle)


def body(
    q_latent,
    w_qnope,
    w_qrope,
    w_uk,
    w_uv,
    w_out,
    cache_latent,
    cache_rope,
    new_latent,
    new_rope,
    lengths,
    page_table,
):
    rows = q_latent.shape[0]
    heads = w_uk.shape[0]
    own = page_table.shape[0]
    width_all = w_out.shape[2]
    dp_count = lax.axis_size("dp")
    sources = lax.axis_size("head")
    depth = w_out.shape[0] * w_out.shape[1]

    head = lax.axis_index("head")
    y = head // Z
    cos, sin = angles(lengths, cache_rope.shape[1])
    y_scalar = y.reshape(1)
    flat = w_out.reshape(depth, width_all)
    both, *cuts = prepare(y_scalar, w_qnope, w_qrope, flat)
    ahead, behind, beside = shift_dp(both, 1, 0), shift_dp(both, -1, 0), shift_dp(both, 0, 1)
    cuts[1] = shift_y(cuts[1], 2)
    own_lengths = lax.dynamic_slice_in_dim(lengths, head * own, own)
    latent, uk = arrange(piece_places(), q_latent, w_uk)
    ahead, behind, beside, cuts, cos, sin, latent, uk, own_lengths = lax.optimization_barrier(
        (ahead, behind, beside, cuts, cos, sin, latent, uk, own_lengths)
    )
    far = shift_dp(ahead, 1, 0)
    ahead_beside, behind_beside = shift_dp(ahead, 0, 1), shift_dp(behind, 0, 1)
    cuts[0], cuts[2] = shift_y(cuts[0], 1), shift_y(cuts[2], 3)
    far, cuts, ahead_beside, behind_beside = lax.optimization_barrier(
        (far, cuts, ahead_beside, behind_beside)
    )
    pieces = [both, ahead, behind, far, beside]
    pieces += [ahead_beside, behind_beside, shift_dp(far, 0, 1)]
    cuts, pieces = lax.optimization_barrier((cuts, pieces))
    panel = lax.all_gather(stack(y_scalar, flat, cuts), "dp", axis=0)
    query = project(latent, pieces, uk, cos, sin)
    query = query.reshape(sources, own * heads, query.shape[1])
    query = lax.all_to_all(query, "head", 0, 0, tiled=True).reshape(rows * heads, -1)
    attn = attend(
        own_lengths, page_table, query, heads, new_latent, new_rope, cache_latent, cache_rope
    )
    attn = attn.reshape(sources, own * heads, attn.shape[1])
    attn = lax.all_to_all(attn, "head", 0, 0, tiled=True).reshape(rows * heads, -1)
    values = project_values(attn, w_uv, dp_count)
    values = jnp.broadcast_to(values[None], (Y,) + values.shape)
    values = lax.all_to_all(values, "head", 0, 0, tiled=True, axis_index_groups=Y_GROUPS)
    term = mix(values, panel, Z)
    term = lax.all_to_all(term, "head", 0, 0, tiled=True, axis_index_groups=Z_GROUPS)
    return finish(term)


def solution(mesh):
    in_specs = (
        P("dp", None),
        P("dp", "head"),
        P("dp", "head"),
        P("head", None, None),
        P("head", None, None),
        P("head", "dp", None),
        P(("dp", "head"), None, None),
        P(("dp", "head"), None, None),
        P(("dp", "head"), None),
        P(("dp", "head"), None),
        P("dp"),
        P(("dp", "head"), None),
    )
    out_specs = P("dp", "head")
    return jax.shard_map(body, mesh=mesh, in_specs=in_specs, out_specs=out_specs, check_vma=False)
```
